128 devices in a mesh: depth: 8 (over y, core), tile: 16 (over x, z).
Axes of the slice: x: 4, y: 4, z: 4, core: 2. Of those that a mesh axis runs over, the one named last changes fastest.
Arguments:
- fields: float32 [2, 256, 256, 1024], P(None, 'depth', 'tile'), may hold values from -6 to 6
- colour_palette: float32 [3, 16], replicated, may hold values from 0.05 to 1
- opacity_palette: float32 [16], replicated, may hold values from 0.2 to 3
- tf_index: int32 [256], replicated, may hold values from 0 to 15
Outputs:
- image: float32 [4, 256, 1024], P(None, 'tile', 'depth')
The draws below stay inside these ranges and needn't reach their ends.
All inputs are finite; a program needn't handle non-finite values.
Results may differ from the reference program's by a relative error of at most 0.0003.
Values sent between devices are 32-bit elements; how exact they have to be, the bound alone decides.
A program may use at most 64 MiB of HBM per device.

```python
import math
import jax
import jax.numpy as jnp
import numpy as np
from jax import lax

TX = 16
NY = 1024
BINS = 256
PALETTE = 16
NX = 256
NZ = 256


def touch_ends(array, stream_key, low, top_value):
    extent = array.shape
    place = [jax.random.randint(jax.random.fold_in(stream_key, axis), (), 0, extent[axis]) for axis in range(len(extent))]
    array = array.at[tuple(place)].set(low)
    longest = extent.index(max(extent))
    place[longest] = (place[longest] + 1) % extent[longest]
    return array.at[tuple(place)].set(top_value)


def levels(stream_key, shape, shards, smallest, top_value):
    factor_of, own = 1.0, jax.random.fold_in(stream_key, 6)
    for dim, parts in shards:
        steps = jnp.exp(jax.random.uniform(jax.random.fold_in(own, dim), (parts,), jnp.float32, smallest / len(shards), top_value / len(shards)))
        factor_of = factor_of * jnp.repeat(steps, shape[dim] // parts).reshape([-1 if axis == dim else 1 for axis in range(len(shape))])
    return factor_of


def gaussian(own_key, dims, scale, limit, pieces=(), held_as=jnp.bfloat16):
    values = jax.random.normal(own_key, dims, jnp.float32) * scale
    if len(pieces) > 0:
        values = levels(own_key, dims, pieces, -0.22, 0.18) * values
    return jnp.clip(values, min=-limit, max=limit).astype(held_as)


def setup_inputs(seed: int = 0) -> dict:
    arg_keys = jax.random.split(jax.random.key(seed), 5)
    return {
        "fields": gaussian(arg_keys[0], (2, NZ, NX, NY), 1.0, 6.0, ((1, 8), (2, 16)), jnp.float32),
        "colour_palette": jnp.clip(jax.random.uniform(arg_keys[1], (3, PALETTE), jnp.float32, 0.05, 1.0), 0.05, 1.0),
        "opacity_palette": jnp.clip(jnp.exp(jax.random.uniform(arg_keys[2], (PALETTE,), jnp.float32, math.log(0.2), math.log(3.0))), 0.2, 3.0),
        "tf_index": touch_ends(jax.random.randint(arg_keys[3], (BINS,), 0, PALETTE), jax.random.fold_in(arg_keys[3], 1), 0, PALETTE - 1).astype(jnp.int32),
    }


taps_offset = np.arange(-4.0, 5.0)
gauss_bell = np.exp(-taps_offset ** 2 / 8.0)
smooth_taps = tuple((float(weight) for weight in gauss_bell / np.sqrt(np.sum(gauss_bell ** 2))))
slope_raw = taps_offset * gauss_bell
slope_taps = tuple((float(weight) for weight in slope_raw / np.sqrt(np.sum(slope_raw ** 2))))

def filter_axis(field, taps, axis):
    count = field.shape[axis] - (len(taps) - 1)
    total = taps[0] * lax.slice_in_dim(field, 0, count, axis=axis)
    for offset in range(1, len(taps)):
        total = total + taps[offset] * lax.slice_in_dim(field, offset, offset + count, axis=axis)
    return total

def smooth_three(field, first):
    for axis in range(first, first + 3):
        field = filter_axis(field, smooth_taps, axis)
    return field

def slopes(smooth_a):
    core = smooth_a[4:-4, 4:-4, 4:-4]
    grad_z = filter_axis(smooth_a[:, 4:-4, 4:-4], slope_taps, 0)
    grad_x = filter_axis(smooth_a[4:-4, :, 4:-4], slope_taps, 1)
    grad_y = filter_axis(smooth_a[4:-4, 4:-4, :], slope_taps, 2)
    return (core, grad_z, grad_x, grad_y)

def shade_march(smooth_a, smooth_b, grad_z, grad_x, grad_y, table, depth_total):
    bins = table.shape[1]
    level = (bins - 1) * jax.nn.sigmoid(1.5 * smooth_a)
    bin_index = jnp.clip(jnp.floor(level).astype(jnp.int32), 0, bins - 2)
    fraction = level - bin_index.astype(level.dtype)
    lower = jnp.take(table, bin_index, axis=1)
    upper = jnp.take(table, bin_index + 1, axis=1)
    looked = lower * (1.0 - fraction) + upper * fraction
    facing = jnp.abs(0.26726 * grad_z + 0.53452 * grad_x + 0.80178 * grad_y)
    length = jnp.sqrt(jnp.maximum(grad_z * grad_z + grad_x * grad_x + grad_y * grad_y, 0.1))
    shade = 0.3 + 0.7 * facing / length
    optical = 1.5 * (2.0 / depth_total) * looked[3] * jax.nn.sigmoid(2.0 * smooth_b)
    running = jnp.cumsum(optical, axis=0)
    total = running[-1]
    before = running - optical
    weight = jnp.exp(-before) * -jnp.expm1(-optical)
    colour = lax.optimization_barrier(jnp.sum(weight[None] * looked[:3] * shade[None], axis=1))
    return jnp.concatenate([colour, jnp.exp(-total)[None]], axis=0)

def reference(fields, colour_palette, opacity_palette, tf_index):
    table = jnp.concatenate([jnp.take(colour_palette, tf_index, axis=1), jnp.take(opacity_palette, tf_index)[None]], axis=0)
    padded = jnp.pad(fields, ((0, 0), (8, 8), (8, 8), (8, 8)))
    depth_pos = jnp.arange(NZ + 8, dtype=jnp.int32) - 4
    depth_ok = (depth_pos >= 0) & (depth_pos < NZ)
    column_pos = jnp.arange(NY + 8, dtype=jnp.int32) - 4
    column_ok = (column_pos >= 0) & (column_pos < NY)

    def one_strip(strip):
        piece = lax.dynamic_slice_in_dim(padded, (strip * TX).astype(jnp.int32), TX + 16, axis=2)
        smooth_a = smooth_three(piece[0], 0)
        row_pos = strip * TX - 4 + jnp.arange(TX + 8, dtype=jnp.int32)
        row_ok = (row_pos >= 0) & (row_pos < NX)
        inside = depth_ok[:, None, None] & row_ok[None, :, None] & column_ok[None, None, :]
        smooth_a = jnp.where(inside, smooth_a, jnp.float32(0.0))
        smooth_b = smooth_three(piece[1, 4:-4, 4:-4, 4:-4], 0)
        core, grad_z, grad_x, grad_y = slopes(smooth_a)
        return shade_march(core, smooth_b, grad_z, grad_x, grad_y, table, NZ)
    strips = lax.map(one_strip, jnp.arange(NX // TX, dtype=jnp.int32))
    return jnp.transpose(strips, (1, 0, 2, 3)).reshape(4, NX, NY)
```

```python
import functools

import jax
import jax.numpy as jnp
import numpy as np
from jax import lax
from jax.experimental import pallas as pl
from jax.experimental.pallas import tpu as pltpu
from jax.sharding import PartitionSpec as P

MESH = pl.DeviceIdType.MESH
W = 128

offsets = np.arange(-4.0, 5.0)
bell = np.exp(-(offsets**2) / 8.0)
bell_norm = float(np.sqrt(np.sum(bell**2)))
slope_norm = float(np.sqrt(np.sum((offsets * bell) ** 2)))
RATIO = [float(np.exp(-(k * k) / 8.0)) for k in range(5)]
SMOOTH_SCALE = float(bell_norm**-3)
SLOPE = [0.0] + [float(k * RATIO[k] / RATIO[1]) for k in range(1, 5)]
SLOPE_SCALE = float(RATIO[1] / slope_norm)
LENGTH_FLOOR = float(0.1 / (SLOPE_SCALE * SMOOTH_SCALE) ** 2)


def even_sum(centre, pairs):
    total = centre
    for k in range(1, 5):
        low, high = pairs(k)
        total = total + RATIO[k] * (low + high)
    return total


def odd_sum(pairs):
    total = None
    for k in range(1, 5):
        low, high = pairs(k)
        term = high - low
        total = term if total is None else total + SLOPE[k] * term
    return total


def column_pairs(prev, cur, nxt):
    lane = lax.broadcasted_iota(jnp.int32, cur.shape, 1)

    def pairs(k):
        low = pltpu.roll(jnp.where(lane < W - k, cur, prev), k, 1)
        high = pltpu.roll(jnp.where(lane >= k, cur, nxt), W - k, 1)
        return low, high

    return pairs


def kernel(
    n_depth, n_tile, parts,
    fields, cpal, opal, tf, out,
    F0, F1, E0, X0, S, Y1, Z1, C, PT, R, tab, idx,
    load_sem, s_send, s_recv, f_send, f_recv,
):
    _, NZL, NXL, NYL = fields.shape
    NC = NYL // W
    d = lax.axis_index("depth")
    t = lax.axis_index("tile")
    d_up, d_dn = lax.rem(d + n_depth - 1, n_depth), lax.rem(d + 1, n_depth)
    t_up, t_dn = lax.rem(t + n_tile - 1, n_tile), lax.rem(t + 1, n_tile)
    comm = "comm" in parts

    def load(field, c):
        buf = (F0, F1)[field]
        return pltpu.make_async_copy(
            fields.at[field, :, :, c * W : (c + 1) * W], buf.at[c + 1], load_sem.at[field, c]
        )

    if comm:
        barrier = pltpu.get_barrier_semaphore()
        for where in ((d, t_up), (d, t_dn)):
            pl.semaphore_signal(barrier, inc=1, device_id=where, device_id_type=MESH)
        for step in range(1, n_depth):
            pl.semaphore_signal(
                barrier, inc=1, device_id=(lax.rem(d + step, n_depth), t), device_id_type=MESH
            )
    for field in range(2):
        for c in range(NC):
            load(field, c).start()

    zeros = jnp.zeros((8, W), jnp.float32)
    for j in range(4):
        tab[j] = zeros
    for j in range(3):
        tab[j, :, 0:16] = jnp.broadcast_to(cpal[j : j + 1, :], (8, 16))
    tab[3, :, 0:16] = jnp.broadcast_to(opal[...].reshape(1, 16), (8, 16))
    whole = tf[...].reshape(2, W)
    low_tf = jnp.broadcast_to(whole[0:1], (8, W))
    high_tf = jnp.broadcast_to(whole[1:2], (8, W))
    lane8 = lax.broadcasted_iota(jnp.int32, (8, W), 1)
    idx[0] = low_tf + 16 * pltpu.roll(jnp.where(lane8 >= 1, low_tf, high_tf), W - 1, 1)
    idx[1] = high_tf + 16 * pltpu.roll(high_tf, W - 1, 1)

    for buf in (F0, F1):
        buf[0] = jnp.zeros_like(buf[0])
        buf[NC + 1] = jnp.zeros_like(buf[NC + 1])
    S[0] = jnp.zeros_like(S[0])
    S[NC + 1] = jnp.zeros_like(S[NC + 1])

    if comm:
        pl.semaphore_wait(barrier, n_depth + 1)

    def remote(kind, side, c, src, dst, where):
        return pltpu.make_async_remote_copy(
            src_ref=src,
            dst_ref=dst,
            send_sem=s_send.at[kind, side, c],
            recv_sem=s_recv.at[kind, side, c],
            device_id=where,
            device_id_type=MESH,
        )

    def copies(kind, c):
        if kind == 0:
            return (
                remote(0, 0, c, E0.at[c, :, 16:24], E0.at[c, :, 0:8], (d, t_dn)),
                remote(0, 1, c, E0.at[c, :, 8:16], E0.at[c, :, 24:32], (d, t_up)),
            )
        if kind == 1:
            return (
                remote(1, 0, c, X0.at[c, 32:40], X0.at[c, 0:8], (d_dn, t)),
                remote(1, 1, c, X0.at[c, 8:16], X0.at[c, 40:48], (d_up, t)),
            )
        if kind == 2:
            return (
                remote(2, 0, c, Y1.at[c, 32:36], Y1.at[c, 0:4], (d_dn, t)),
                remote(2, 1, c, Y1.at[c, 4:8], Y1.at[c, 36:40], (d_up, t)),
            )
        return (
            remote(3, 0, c, Z1.at[c, :, 20:24], Z1.at[c, :, 4:8], (d, t_dn)),
            remote(3, 1, c, Z1.at[c, :, 8:12], Z1.at[c, :, 24:28], (d, t_up)),
        )

    def send(kind, c):
        if comm:
            for copy in copies(kind, c):
                copy.start()

    def receive(kind, c):
        if comm:
            for copy in copies(kind, c):
                copy.wait_recv()

    def final_copy(c, source, target):
        return pltpu.make_async_remote_copy(
            src_ref=PT.at[c],
            dst_ref=R.at[source],
            send_sem=f_send.at[c],
            recv_sem=f_recv.at[source],
            device_id=(target, t),
            device_id_type=MESH,
        )

    def clear(cond, ref, *where):
        @pl.when(cond)
        def _():
            part = ref.at[where]
            part[...] = jnp.zeros(part.shape, jnp.float32)

    def columns_smooth(buf, c, p):
        prev, cur, nxt = buf[c, p], buf[c + 1, p], buf[c + 2, p]
        return even_sum(cur, column_pairs(prev, cur, nxt))

    def stage_a0(c, _):
        @pl.when(c < NC - 1)
        def _():
            pltpu.make_async_copy(
                fields.at[0, :, :, 0:W], F0.at[c + 2], load_sem.at[0, c + 1]
            ).wait()

        def body(p, _):
            E0[c, p, 8:24] = columns_smooth(F0, c, p)
            return 0

        lax.fori_loop(0, NZL, body, 0, unroll=2)
        send(0, c)
        return 0

    def stage_a1(c, _):
        @pl.when(c < NC - 1)
        def _():
            pltpu.make_async_copy(
                fields.at[0, :, :, 0:W], F1.at[c + 2], load_sem.at[1, c + 1]
            ).wait()

        def body(p, _):
            Y1[c, p + 4] = columns_smooth(F1, c, p)
            return 0

        lax.fori_loop(0, NZL, body, 0, unroll=2)
        send(2, c)
        return 0

    def stage_b(c):
        receive(0, c)
        clear(t == 0, E0, c, slice(None), slice(0, 8))
        clear(t == n_tile - 1, E0, c, slice(None), slice(24, 32))

        def body(p, _):
            def pairs(k):
                return E0[c, p, 4 - k : 28 - k], E0[c, p, 4 + k : 28 + k]

            X0[c, p + 8] = even_sum(E0[c, p, 4:28], pairs)
            return 0

        lax.fori_loop(0, NZL, body, 0, unroll=2)
        clear(t == 0, X0, c, slice(8, 40), slice(0, 4))
        clear(t == n_tile - 1, X0, c, slice(8, 40), slice(20, 24))
        send(1, c)

    def stage_c(c):
        receive(1, c)
        clear(d == 0, X0, c, slice(0, 8))
        clear(d == n_depth - 1, X0, c, slice(40, 48))

        def body(g, _):
            for r in range(0, 24, 8):
                planes = [X0[c, g * 8 + i, r : r + 8] for i in range(16)]
                for i in range(8):
                    S[c + 1, g * 8 + i, r : r + 8] = even_sum(
                        planes[i + 4], lambda k: (planes[i + 4 - k], planes[i + 4 + k])
                    )
            return 0

        lax.fori_loop(0, (NZL + 8) // 8, body, 0)
        clear(d == 0, S, c + 1, slice(0, 4))
        clear(d == n_depth - 1, S, c + 1, slice(36, 40))

    def stage_b1(c):
        receive(2, c)
        clear(d == 0, Y1, c, slice(0, 4))
        clear(d == n_depth - 1, Y1, c, slice(36, 40))

        def body(g, _):
            for r in range(0, 16, 8):
                planes = [Y1[c, g * 8 + i, r : r + 8] for i in range(16)]
                for i in range(8):
                    Z1[c, g * 8 + i, r + 8 : r + 16] = even_sum(
                        planes[i + 4], lambda k: (planes[i + 4 - k], planes[i + 4 + k])
                    )
            return 0

        lax.fori_loop(0, NZL // 8, body, 0)
        send(3, c)

    def gather(table, where):
        return jnp.take_along_axis(table, where, axis=1, mode="promise_in_bounds")

    def stage_d(c):
        def body(p, _):
            for r in (0, 8):
                centre = S[c + 1, p + 4, r + 4 : r + 12]
                prev = S[c, p + 4, r + 4 : r + 12]
                nxt = S[c + 2, p + 4, r + 4 : r + 12]
                grad_z = odd_sum(
                    lambda k: (
                        S[c + 1, p + 4 - k, r + 4 : r + 12],
                        S[c + 1, p + 4 + k, r + 4 : r + 12],
                    )
                )
                grad_x = odd_sum(
                    lambda k: (
                        S[c + 1, p + 4, r + 4 - k : r + 12 - k],
                        S[c + 1, p + 4, r + 4 + k : r + 12 + k],
                    )
                )
                grad_y = odd_sum(column_pairs(prev, centre, nxt))
                facing = jnp.abs(0.26726 * grad_z + 0.53452 * grad_x + 0.80178 * grad_y)
                square = grad_z * grad_z + grad_x * grad_x + grad_y * grad_y
                shade = 0.3 + 0.7 * facing * lax.rsqrt(jnp.maximum(square, LENGTH_FLOOR))
                level = 127.5 + 127.5 * jnp.tanh((0.75 * SMOOTH_SCALE) * centre)
                bin_index = jnp.minimum(level.astype(jnp.int32), 254)
                fraction = level - bin_index.astype(jnp.float32)
                near = bin_index & 127
                pair = jnp.where(bin_index < 128, gather(idx[0], near), gather(idx[1], near))
                lower, upper = pair & 15, pair >> 4
                for j in range(4):
                    low = gather(tab[j], lower)
                    looked = low + (gather(tab[j], upper) - low) * fraction
                    C[c, j, p, r : r + 8] = looked if j == 3 else looked * shade
            return 0

        lax.fori_loop(0, NZL, body, 0)

    def stage_e(c, _):
        receive(3, c)
        clear(t == 0, Z1, c, slice(None), slice(4, 8))
        clear(t == n_tile - 1, Z1, c, slice(None), slice(24, 28))

        def body(p, carry):
            through, red, green, blue = carry

            def pairs(k):
                return Z1[c, p, 8 - k : 24 - k], Z1[c, p, 8 + k : 24 + k]

            smooth = even_sum(Z1[c, p, 8:24], pairs)
            gate = 0.5 + 0.5 * jnp.tanh(SMOOTH_SCALE * smooth)
            optical = (-1.5 * 2.0 / (NZL * n_depth)) * C[c, 3, p] * gate
            kept = through * jnp.exp(optical)
            weight = through - kept
            return (
                kept,
                red + weight * C[c, 0, p],
                green + weight * C[c, 1, p],
                blue + weight * C[c, 2, p],
            )

        none = jnp.zeros((NXL, W), jnp.float32)
        through, red, green, blue = lax.fori_loop(
            0, NZL, body, (jnp.ones((NXL, W), jnp.float32), none, none, none), unroll=2
        )

        def put(ref, where):
            for j, value in enumerate((red, green, blue, through)):
                ref[where, j] = value

        @pl.when(c == d)
        def _():
            put(R, d)

        @pl.when(c != d)
        def _():
            put(PT, c)
            if comm:
                final_copy(c, d, c).start()

        return 0

    load(0, 0).wait()
    if "a" in parts:
        lax.fori_loop(0, NC, stage_a0, 0)
    load(1, 0).wait()
    if "a" in parts:
        lax.fori_loop(0, NC, stage_a1, 0)
    else:
        for field in range(2):
            for c in range(1, NC):
                load(field, c).wait()

    def middle(i, _):
        @pl.when(i < NC)
        def _():
            if "b" in parts:
                stage_b(i)
            if "b1" in parts:
                stage_b1(i)

        @pl.when((i >= 1) & (i < NC + 1))
        def _():
            if "c" in parts:
                stage_c(i - 1)

        @pl.when(i >= 2)
        def _():
            if "d" in parts:
                stage_d(i - 2)

        return 0

    lax.fori_loop(0, NC + 2, middle, 0)
    if "e" in parts:
        lax.fori_loop(0, NC, stage_e, 0)

    if comm:

        def wait_final(i, _):
            @pl.when(i != d)
            def _():
                final_copy(i, i, i).wait_recv()

            return 0

        lax.fori_loop(0, n_depth, wait_final, 0)
    through, red, green, blue = R[0, 3], R[0, 0], R[0, 1], R[0, 2]
    for i in range(1, n_depth):
        red = red + through * R[i, 0]
        green = green + through * R[i, 1]
        blue = blue + through * R[i, 2]
        through = through * R[i, 3]
    for j, value in enumerate((red, green, blue, through)):
        out[j] = value

    if comm:

        def drain(c, _):
            for kind in range(4):
                for copy in copies(kind, c):
                    copy.wait_send()

            @pl.when(c != d)
            def _():
                final_copy(c, d, c).wait_send()

            return 0

        lax.fori_loop(0, NC, drain, 0)


ALL = ("comm", "a", "b", "b1", "c", "d", "e")


def local(n_depth, n_tile, parts, fields, colour_palette, opacity_palette, tf_index):
    _, planes, rows, columns = fields.shape
    chunks = columns // W
    f32 = jnp.float32
    vmem = pl.BlockSpec(memory_space=pltpu.VMEM)
    return pl.pallas_call(
        functools.partial(kernel, n_depth, n_tile, parts),
        out_shape=jax.ShapeDtypeStruct((4, rows, W), f32),
        in_specs=[pl.BlockSpec(memory_space=pl.ANY), vmem, vmem, vmem],
        out_specs=vmem,
        scratch_shapes=[
            pltpu.VMEM((chunks + 2, planes, rows, W), f32),
            pltpu.VMEM((chunks + 2, planes, rows, W), f32),
            pltpu.VMEM((chunks, planes, rows + 16, W), f32),
            pltpu.VMEM((chunks, planes + 16, rows + 8, W), f32),
            pltpu.VMEM((chunks + 2, planes + 8, rows + 8, W), f32),
            pltpu.VMEM((chunks, planes + 8, rows, W), f32),
            pltpu.VMEM((chunks, planes, rows + 16, W), f32),
            pltpu.VMEM((chunks, 4, planes, rows, W), f32),
            pltpu.VMEM((chunks, 4, rows, W), f32),
            pltpu.VMEM((chunks, 4, rows, W), f32),
            pltpu.VMEM((4, 8, W), f32),
            pltpu.VMEM((2, 8, W), jnp.int32),
            pltpu.SemaphoreType.DMA((2, chunks)),
            pltpu.SemaphoreType.DMA((4, 2, chunks)),
            pltpu.SemaphoreType.DMA((4, 2, chunks)),
            pltpu.SemaphoreType.DMA((chunks,)),
            pltpu.SemaphoreType.DMA((chunks,)),
        ],
        compiler_params=pltpu.CompilerParams(
            collective_id=0 if "comm" in parts else None,
            has_side_effects=True,
            vmem_limit_bytes=56 * 1024 * 1024,
        ),
    )(fields, colour_palette, opacity_palette, tf_index)


def solution(mesh, parts=ALL):
    placed = (P(None, "depth", "tile", None), P(), P(), P())
    return jax.shard_map(
        functools.partial(local, mesh.shape["depth"], mesh.shape["tile"], parts),
        mesh=mesh,
        in_specs=placed,
        out_specs=P(None, "tile", "depth"),
        check_vma=False,
    )
```

```python
import functools

import jax
import jax.numpy as jnp
import numpy as np
from jax import lax
from jax.experimental import pallas as pl
from jax.experimental.pallas import tpu as pltpu
from jax.sharding import PartitionSpec as P

MESH = pl.DeviceIdType.MESH
W = 128

offsets = np.arange(-4.0, 5.0)
bell = np.exp(-(offsets**2) / 8.0)
bell_norm = float(np.sqrt(np.sum(bell**2)))
slope_norm = float(np.sqrt(np.sum((offsets * bell) ** 2)))
RATIO = [float(np.exp(-(k * k) / 8.0)) for k in range(5)]
SMOOTH_SCALE = float(bell_norm**-3)
SLOPE = [0.0] + [float(k * RATIO[k] / RATIO[1]) for k in range(1, 5)]
SLOPE_SCALE = float(RATIO[1] / slope_norm)
LENGTH_FLOOR = float(0.1 / (SLOPE_SCALE * SMOOTH_SCALE) ** 2)


def even_sum(centre, pairs):
    total = centre
    for k in range(1, 5):
        low, high = pairs(k)
        total = total + RATIO[k] * (low + high)
    return total


def odd_sum(pairs):
    total = None
    for k in range(1, 5):
        low, high = pairs(k)
        term = high - low
        total = term if total is None else total + SLOPE[k] * term
    return total


def tap_matrices(taps, odd):
    source = lax.broadcasted_iota(jnp.int32, (W, W), 0)
    target = lax.broadcasted_iota(jnp.int32, (W, W), 1)
    halves = []
    for start in (source, jnp.where(source < 4, source + W, source - W)):
        distance = start - target
        matrix = jnp.zeros((W, W), jnp.float32)
        for k in range(-4, 5):
            tap = -taps[-k] if odd and k < 0 else taps[abs(k)]
            matrix = jnp.where(distance == k, jnp.float32(tap), matrix)
        if start is not source:
            matrix = jnp.where((source < 4) | (source >= W - 4), matrix, 0.0)
        high = matrix.astype(jnp.bfloat16)
        low = (matrix - high.astype(jnp.float32)).astype(jnp.bfloat16)
        halves += [high, high, low]
    return jnp.concatenate(halves, axis=0)


def column_filter(prev, cur, nxt, matrix):
    lane = lax.broadcasted_iota(jnp.int32, cur.shape, 1)
    pieces = []
    for values in (cur, jnp.where(lane < 4, nxt, prev)):
        high = values.astype(jnp.bfloat16)
        low = (values - high.astype(jnp.float32)).astype(jnp.bfloat16)
        pieces += [high, low, high]
    return jnp.dot(
        jnp.concatenate(pieces, axis=1), matrix, preferred_element_type=jnp.float32
    )


def column_pairs(prev, cur, nxt):
    lane = lax.broadcasted_iota(jnp.int32, cur.shape, 1)

    def pairs(k):
        low = pltpu.roll(jnp.where(lane < W - k, cur, prev), k, 1)
        high = pltpu.roll(jnp.where(lane >= k, cur, nxt), W - k, 1)
        return low, high

    return pairs


def kernel(
    n_depth, n_tile, parts,
    fields, cpal, opal, tf, out,
    F0, F1, E0, X0, S, Y1, Z1, C, PT, R, tab, idx, taps,
    load_sem, s_send, s_recv, f_send, f_recv,
):
    _, NZL, NXL, NYL = fields.shape
    NC = NYL // W
    d = lax.axis_index("depth")
    t = lax.axis_index("tile")
    d_up, d_dn = lax.rem(d + n_depth - 1, n_depth), lax.rem(d + 1, n_depth)
    t_up, t_dn = lax.rem(t + n_tile - 1, n_tile), lax.rem(t + 1, n_tile)
    comm = "comm" in parts

    def load(field, c):
        buf = (F0, F1)[field]
        return pltpu.make_async_copy(
            fields.at[field, :, :, c * W : (c + 1) * W], buf.at[c + 1], load_sem.at[field, c]
        )

    if comm:
        barrier = pltpu.get_barrier_semaphore()
        for where in ((d, t_up), (d, t_dn)):
            pl.semaphore_signal(barrier, inc=1, device_id=where, device_id_type=MESH)
        for step in range(1, n_depth):
            pl.semaphore_signal(
                barrier, inc=1, device_id=(lax.rem(d + step, n_depth), t), device_id_type=MESH
            )
    for field in range(2):
        for c in range(NC):
            load(field, c).start()

    entry = lax.broadcasted_iota(jnp.int32, (8, 16), 0)
    column = lax.broadcasted_iota(jnp.int32, (8, 16), 1)
    for j in range(4):
        row = opal[...].reshape(1, 16) if j == 3 else cpal[j : j + 1, :]
        for h in range(2):
            picked = jnp.where(column == entry + 8 * h, jnp.broadcast_to(row, (8, 16)), 0.0)
            tab[j, h] = jnp.broadcast_to(jnp.sum(picked, axis=1, keepdims=True), (8, W))
    whole = tf[...].reshape(2, W)
    low_tf = jnp.broadcast_to(whole[0:1], (8, W))
    high_tf = jnp.broadcast_to(whole[1:2], (8, W))
    lane8 = lax.broadcasted_iota(jnp.int32, (8, W), 1)
    low_next = pltpu.roll(jnp.where(lane8 >= 1, low_tf, high_tf), W - 1, 1)
    high_next = pltpu.roll(high_tf, W - 1, 1)
    idx[...] = low_tf + 16 * low_next + 256 * high_tf + 4096 * high_next

    taps[0] = tap_matrices(RATIO, False)
    taps[1] = tap_matrices(SLOPE, True)
    for buf in (F0, F1):
        buf[0] = jnp.zeros_like(buf[0])
        buf[NC + 1] = jnp.zeros_like(buf[NC + 1])
    S[0] = jnp.zeros_like(S[0])
    S[NC + 1] = jnp.zeros_like(S[NC + 1])

    if comm:
        pl.semaphore_wait(barrier, n_depth + 1)

    def remote(kind, side, c, src, dst, where):
        return pltpu.make_async_remote_copy(
            src_ref=src,
            dst_ref=dst,
            send_sem=s_send.at[kind, side, c],
            recv_sem=s_recv.at[kind, side, c],
            device_id=where,
            device_id_type=MESH,
        )

    def copies(kind, c):
        if kind == 0:
            return (
                remote(0, 0, c, E0.at[c, :, 16:24], E0.at[c, :, 0:8], (d, t_dn)),
                remote(0, 1, c, E0.at[c, :, 8:16], E0.at[c, :, 24:32], (d, t_up)),
            )
        if kind == 1:
            return (
                remote(1, 0, c, X0.at[c, 32:40], X0.at[c, 0:8], (d_dn, t)),
                remote(1, 1, c, X0.at[c, 8:16], X0.at[c, 40:48], (d_up, t)),
            )
        if kind == 2:
            return (
                remote(2, 0, c, Y1.at[c, 32:36], Y1.at[c, 0:4], (d_dn, t)),
                remote(2, 1, c, Y1.at[c, 4:8], Y1.at[c, 36:40], (d_up, t)),
            )
        return (
            remote(3, 0, c, Z1.at[c, :, 20:24], Z1.at[c, :, 4:8], (d, t_dn)),
            remote(3, 1, c, Z1.at[c, :, 8:12], Z1.at[c, :, 24:28], (d, t_up)),
        )

    def send(kind, c):
        if comm:
            for copy in copies(kind, c):
                copy.start()

    def receive(kind, c):
        if comm:
            for copy in copies(kind, c):
                copy.wait_recv()

    def final_copy(c, source, target):
        return pltpu.make_async_remote_copy(
            src_ref=PT.at[c],
            dst_ref=R.at[source],
            send_sem=f_send.at[c],
            recv_sem=f_recv.at[source],
            device_id=(target, t),
            device_id_type=MESH,
        )

    def clear(cond, ref, *where):
        @pl.when(cond)
        def _():
            part = ref.at[where]
            part[...] = jnp.zeros(part.shape, jnp.float32)

    MB = 16

    def columns_smooth(buf, c, p):
        prev, cur, nxt = (
            buf[c + i, pl.ds(p, MB)].reshape(MB * NXL, W) for i in range(3)
        )
        return column_filter(prev, cur, nxt, taps[0]).reshape(MB, NXL, W)

    def stage_a0(c, _):
        @pl.when(c < NC - 1)
        def _():
            pltpu.make_async_copy(
                fields.at[0, :, :, 0:W], F0.at[c + 2], load_sem.at[0, c + 1]
            ).wait()

        def body(p, _):
            E0[c, pl.ds(p * MB, MB), 8:24] = columns_smooth(F0, c, p * MB)
            return 0

        lax.fori_loop(0, NZL // MB, body, 0)
        send(0, c)
        return 0

    def stage_a1(c, _):
        @pl.when(c < NC - 1)
        def _():
            pltpu.make_async_copy(
                fields.at[0, :, :, 0:W], F1.at[c + 2], load_sem.at[1, c + 1]
            ).wait()

        def body(p, _):
            Y1[c, pl.ds(p * MB + 4, MB)] = columns_smooth(F1, c, p * MB)
            return 0

        lax.fori_loop(0, NZL // MB, body, 0)
        send(2, c)
        return 0

    def stage_b(c):
        receive(0, c)
        clear(t == 0, E0, c, slice(None), slice(0, 8))
        clear(t == n_tile - 1, E0, c, slice(None), slice(24, 32))

        def body(p, _):
            def pairs(k):
                return E0[c, p, 4 - k : 28 - k], E0[c, p, 4 + k : 28 + k]

            X0[c, p + 8] = even_sum(E0[c, p, 4:28], pairs)
            return 0

        lax.fori_loop(0, NZL, body, 0, unroll=2)
        clear(t == 0, X0, c, slice(8, 40), slice(0, 4))
        clear(t == n_tile - 1, X0, c, slice(8, 40), slice(20, 24))
        send(1, c)

    def stage_c(c):
        receive(1, c)
        clear(d == 0, X0, c, slice(0, 8))
        clear(d == n_depth - 1, X0, c, slice(40, 48))

        def body(g, _):
            for r in range(0, 24, 8):
                planes = [X0[c, g * 8 + i, r : r + 8] for i in range(16)]
                for i in range(8):
                    S[c + 1, g * 8 + i, r : r + 8] = even_sum(
                        planes[i + 4], lambda k: (planes[i + 4 - k], planes[i + 4 + k])
                    )
            return 0

        lax.fori_loop(0, (NZL + 8) // 8, body, 0)
        clear(d == 0, S, c + 1, slice(0, 4))
        clear(d == n_depth - 1, S, c + 1, slice(36, 40))

    def stage_b1(c):
        receive(2, c)
        clear(d == 0, Y1, c, slice(0, 4))
        clear(d == n_depth - 1, Y1, c, slice(36, 40))

        def body(g, _):
            for r in range(0, 16, 8):
                planes = [Y1[c, g * 8 + i, r : r + 8] for i in range(16)]
                for i in range(8):
                    Z1[c, g * 8 + i, r + 8 : r + 16] = even_sum(
                        planes[i + 4], lambda k: (planes[i + 4 - k], planes[i + 4 + k])
                    )
            return 0

        lax.fori_loop(0, NZL // 8, body, 0)
        send(3, c)

    def gather(table, where, axis):
        return jnp.take_along_axis(table, where, axis=axis, mode="promise_in_bounds")

    G, UE = 8, 8
    for part in parts:
        if part[0] == "g":
            G = int(part[1:])
        if part[0] == "u":
            UE = int(part[1:])

    def stage_d(c):
        def slope(p, _):
            prev, cur, nxt = (
                S[c + i, pl.ds(p * MB + 4, MB), 4:20].reshape(MB * NXL, W) for i in range(3)
            )
            C[c, 0, pl.ds(p * MB, MB)] = column_filter(prev, cur, nxt, taps[1]).reshape(MB, NXL, W)
            return 0

        lax.fori_loop(0, NZL // MB, slope, 0)

        def cells(p, r):
            centre = S[c + 1, p + 4, r + 4 : r + 12]
            grad_z = odd_sum(
                lambda k: (
                    S[c + 1, p + 4 - k, r + 4 : r + 12],
                    S[c + 1, p + 4 + k, r + 4 : r + 12],
                )
            )
            grad_x = odd_sum(
                lambda k: (
                    S[c + 1, p + 4, r + 4 - k : r + 12 - k],
                    S[c + 1, p + 4, r + 4 + k : r + 12 + k],
                )
            )
            grad_y = C[c, 0, p, r : r + 8]
            facing = jnp.abs(0.26726 * grad_z + 0.53452 * grad_x + 0.80178 * grad_y)
            square = grad_z * grad_z + grad_x * grad_x + grad_y * grad_y
            shade = 0.3 + 0.7 * facing * lax.rsqrt(jnp.maximum(square, LENGTH_FLOOR))
            level = 127.5 + 127.5 * jnp.tanh((0.75 * SMOOTH_SCALE) * centre)
            bin_index = jnp.minimum(level.astype(jnp.int32), 254)
            fraction = level - bin_index.astype(jnp.float32)
            if "ng" in parts:
                return [fraction, shade, level, shade]
            pair = gather(idx[...], bin_index & 127, 1) >> ((bin_index >> 7) * 8)
            lower, upper = pair & 15, (pair >> 4) & 15
            lower_row, upper_row = lower & 7, upper & 7
            lower_half, upper_half = lower < 8, upper < 8
            found = []
            for j in range(4):
                halves = [tab[j, h] for h in range(2)]
                low, high = (
                    jnp.where(half, gather(halves[0], row, 0), gather(halves[1], row, 0))
                    for half, row in ((lower_half, lower_row), (upper_half, upper_row))
                )
                looked = low + (high - low) * fraction
                found.append(looked if j == 3 else looked * shade)
            return found

        def body(g, _):
            places = [(g * G + i, r) for i in range(G) for r in (0, 8)]
            for (p, r), found in zip(places, [cells(*place) for place in places]):
                for j in range(4):
                    C[c, j, p, r : r + 8] = found[j]
            return 0

        lax.fori_loop(0, NZL // G, body, 0)

    def stage_e(c, _):
        receive(3, c)
        clear(t == 0, Z1, c, slice(None), slice(4, 8))
        clear(t == n_tile - 1, Z1, c, slice(None), slice(24, 28))

        def body(p, carry):
            through, red, green, blue = carry

            def pairs(k):
                return Z1[c, p, 8 - k : 24 - k], Z1[c, p, 8 + k : 24 + k]

            smooth = even_sum(Z1[c, p, 8:24], pairs)
            gate = 0.5 + 0.5 * jnp.tanh(SMOOTH_SCALE * smooth)
            optical = (-1.5 * 2.0 / (NZL * n_depth)) * C[c, 3, p] * gate
            kept = through * jnp.exp(optical)
            weight = through - kept
            return (
                kept,
                red + weight * C[c, 0, p],
                green + weight * C[c, 1, p],
                blue + weight * C[c, 2, p],
            )

        none = jnp.zeros((NXL, W), jnp.float32)
        through, red, green, blue = lax.fori_loop(
            0, NZL, body, (jnp.ones((NXL, W), jnp.float32), none, none, none), unroll=UE
        )

        def put(ref, where):
            for j, value in enumerate((red, green, blue, through)):
                ref[where, j] = value

        @pl.when(c == d)
        def _():
            put(R, d)

        @pl.when(c != d)
        def _():
            put(PT, c)
            if comm:
                final_copy(c, d, c).start()

        return 0

    load(0, 0).wait()
    if "a" in parts:
        lax.fori_loop(0, NC, stage_a0, 0)
    load(1, 0).wait()
    if "a" in parts:
        lax.fori_loop(0, NC, stage_a1, 0)
    else:
        for field in range(2):
            for c in range(1, NC):
                load(field, c).wait()

    def middle(i, _):
        @pl.when(i < NC)
        def _():
            if "b" in parts:
                stage_b(i)
            if "b1" in parts:
                stage_b1(i)

        @pl.when((i >= 1) & (i < NC + 1))
        def _():
            if "c" in parts:
                stage_c(i - 1)

        @pl.when(i >= 2)
        def _():
            if "d" in parts:
                stage_d(i - 2)

        return 0

    lax.fori_loop(0, NC + 2, middle, 0)
    if "e" in parts:
        lax.fori_loop(0, NC, stage_e, 0)

    if comm:

        def wait_final(i, _):
            @pl.when(i != d)
            def _():
                final_copy(i, i, i).wait_recv()

            return 0

        lax.fori_loop(0, n_depth, wait_final, 0)
    through, red, green, blue = R[0, 3], R[0, 0], R[0, 1], R[0, 2]
    for i in range(1, n_depth):
        red = red + through * R[i, 0]
        green = green + through * R[i, 1]
        blue = blue + through * R[i, 2]
        through = through * R[i, 3]
    for j, value in enumerate((red, green, blue, through)):
        out[j] = value

    if comm:

        def drain(c, _):
            for kind in range(4):
                for copy in copies(kind, c):
                    copy.wait_send()

            @pl.when(c != d)
            def _():
                final_copy(c, d, c).wait_send()

            return 0

        lax.fori_loop(0, NC, drain, 0)


ALL = ("comm", "a", "b", "b1", "c", "d", "e")


def local(n_depth, n_tile, parts, fields, colour_palette, opacity_palette, tf_index):
    _, planes, rows, columns = fields.shape
    chunks = columns // W
    f32 = jnp.float32
    vmem = pl.BlockSpec(memory_space=pltpu.VMEM)
    return pl.pallas_call(
        functools.partial(kernel, n_depth, n_tile, parts),
        out_shape=jax.ShapeDtypeStruct((4, rows, W), f32),
        in_specs=[pl.BlockSpec(memory_space=pl.ANY), vmem, vmem, vmem],
        out_specs=vmem,
        scratch_shapes=[
            pltpu.VMEM((chunks + 2, planes, rows, W), f32),
            pltpu.VMEM((chunks + 2, planes, rows, W), f32),
            pltpu.VMEM((chunks, planes, rows + 16, W), f32),
            pltpu.VMEM((chunks, planes + 16, rows + 8, W), f32),
            pltpu.VMEM((chunks + 2, planes + 8, rows + 8, W), f32),
            pltpu.VMEM((chunks, planes + 8, rows, W), f32),
            pltpu.VMEM((chunks, planes, rows + 16, W), f32),
            pltpu.VMEM((chunks, 4, planes, rows, W), f32),
            pltpu.VMEM((chunks, 4, rows, W), f32),
            pltpu.VMEM((chunks, 4, rows, W), f32),
            pltpu.VMEM((4, 2, 8, W), f32),
            pltpu.VMEM((8, W), jnp.int32),
            pltpu.VMEM((2, 6 * W, W), jnp.bfloat16),
            pltpu.SemaphoreType.DMA((2, chunks)),
            pltpu.SemaphoreType.DMA((4, 2, chunks)),
            pltpu.SemaphoreType.DMA((4, 2, chunks)),
            pltpu.SemaphoreType.DMA((chunks,)),
            pltpu.SemaphoreType.DMA((chunks,)),
        ],
        compiler_params=pltpu.CompilerParams(
            collective_id=0 if "comm" in parts else None,
            has_side_effects=True,
            vmem_limit_bytes=56 * 1024 * 1024,
        ),
    )(fields, colour_palette, opacity_palette, tf_index)


def solution(mesh, parts=ALL):
    placed = (P(None, "depth", "tile", None), P(), P(), P())
    return jax.shard_map(
        functools.partial(local, mesh.shape["depth"], mesh.shape["tile"], parts),
        mesh=mesh,
        in_specs=placed,
        out_specs=P(None, "tile", "depth"),
        check_vma=False,
    )
```

```python
import functools

import jax
import jax.numpy as jnp
import numpy as np
from jax import lax
from jax.experimental import pallas as pl
from jax.experimental.pallas import tpu as pltpu
from jax.sharding import PartitionSpec as P

MESH = pl.DeviceIdType.MESH
W = 128
THIRD = {5: (0, 1), 6: (2, 3, 4), 7: (5, 6, 7)}

offsets = np.arange(-4.0, 5.0)
bell = np.exp(-(offsets**2) / 8.0)
bell_norm = float(np.sqrt(np.sum(bell**2)))
slope_norm = float(np.sqrt(np.sum((offsets * bell) ** 2)))
RATIO = [float(np.exp(-(k * k) / 8.0)) for k in range(5)]
SMOOTH_SCALE = float(bell_norm**-3)
SLOPE = [0.0] + [float(k * RATIO[k] / RATIO[1]) for k in range(1, 5)]
SLOPE_SCALE = float(RATIO[1] / slope_norm)
LENGTH_FLOOR = float(0.1 / (SLOPE_SCALE * SMOOTH_SCALE) ** 2)


def even_sum(centre, pairs):
    total = centre
    for k in range(1, 5):
        low, high = pairs(k)
        total = total + RATIO[k] * (low + high)
    return total


def odd_sum(pairs):
    total = None
    for k in range(1, 5):
        low, high = pairs(k)
        term = high - low
        total = term if total is None else total + SLOPE[k] * term
    return total


def tap_matrices(taps, odd):
    source = lax.broadcasted_iota(jnp.int32, (W, W), 0)
    target = lax.broadcasted_iota(jnp.int32, (W, W), 1)
    halves = []
    for start in (source, jnp.where(source < 4, source + W, source - W)):
        distance = start - target
        matrix = jnp.zeros((W, W), jnp.float32)
        for k in range(-4, 5):
            tap = -taps[-k] if odd and k < 0 else taps[abs(k)]
            matrix = jnp.where(distance == k, jnp.float32(tap), matrix)
        if start is not source:
            matrix = jnp.where((source < 4) | (source >= W - 4), matrix, 0.0)
        high = matrix.astype(jnp.bfloat16)
        low = (matrix - high.astype(jnp.float32)).astype(jnp.bfloat16)
        halves += [high, high, low]
    return jnp.concatenate(halves, axis=0)


def column_filter(prev, cur, nxt, matrix):
    lane = lax.broadcasted_iota(jnp.int32, cur.shape, 1)
    pieces = []
    for values in (cur, jnp.where(lane < 4, nxt, prev)):
        high = values.astype(jnp.bfloat16)
        low = (values - high.astype(jnp.float32)).astype(jnp.bfloat16)
        pieces += [high, low, high]
    return jnp.dot(
        jnp.concatenate(pieces, axis=1), matrix, preferred_element_type=jnp.float32
    )


def kernel(
    n_depth, n_tile,
    fields, colour, opacity, entries, out,
    F0, F1, E0, X0, S, Y1, Z1, C, PT, R, tab, idx, taps, cpal, opal, tf,
    load_sem, table_sem, s_send, s_recv, f_send, f_recv,
):
    _, NZL, NXL, NYL = fields.shape
    NC = NYL // W
    d = lax.axis_index("depth")
    t = lax.axis_index("tile")
    d_up, d_dn = lax.rem(d + n_depth - 1, n_depth), lax.rem(d + 1, n_depth)
    t_up, t_dn = lax.rem(t + n_tile - 1, n_tile), lax.rem(t + 1, n_tile)

    def load(field, c):
        buf = (F0, F1)[field]
        return pltpu.make_async_copy(
            fields.at[field, :, :, c * W : (c + 1) * W], buf.at[c + 1], load_sem.at[field, c]
        )

    barrier = pltpu.get_barrier_semaphore()
    beside = ((t > 0, (d, t_up)), (t < n_tile - 1, (d, t_dn)))
    for present, where in beside:

        @pl.when(present)
        def _():
            pl.semaphore_signal(barrier, inc=1, device_id=where, device_id_type=MESH)

    for step in range(1, n_depth):
        pl.semaphore_signal(
            barrier, inc=1, device_id=(lax.rem(d + step, n_depth), t), device_id_type=MESH
        )
    for field in range(2):
        for c in range(NC):
            load(field, c).start()

    small = [
        pltpu.make_async_copy(source, target, table_sem.at[i])
        for i, (source, target) in enumerate(((colour, cpal), (opacity, opal), (entries, tf)))
    ]
    for copy in small:
        copy.start()

    def tables():
        for copy in small:
            copy.wait()
        entry = lax.broadcasted_iota(jnp.int32, (8, 16), 0)
        column = lax.broadcasted_iota(jnp.int32, (8, 16), 1)
        for j in range(4):
            row = opal[...].reshape(1, 16) if j == 3 else cpal[j : j + 1, :]
            for h in range(2):
                picked = jnp.where(column == entry + 8 * h, jnp.broadcast_to(row, (8, 16)), 0.0)
                tab[j, h] = jnp.broadcast_to(jnp.sum(picked, axis=1, keepdims=True), (8, W))
        whole = tf[...].reshape(2, W)
        low_tf = jnp.broadcast_to(whole[0:1], (8, W))
        high_tf = jnp.broadcast_to(whole[1:2], (8, W))
        lane8 = lax.broadcasted_iota(jnp.int32, (8, W), 1)
        low_next = pltpu.roll(jnp.where(lane8 >= 1, low_tf, high_tf), W - 1, 1)
        high_next = pltpu.roll(high_tf, W - 1, 1)
        idx[...] = low_tf + 16 * low_next + 256 * high_tf + 4096 * high_next

    def remote(kind, side, c, src, dst, where):
        return pltpu.make_async_remote_copy(
            src_ref=src,
            dst_ref=dst,
            send_sem=s_send.at[kind, side, c],
            recv_sem=s_recv.at[kind, side, c],
            device_id=where,
            device_id_type=MESH,
        )

    def copies(kind, c):
        if kind == 0:
            return (
                remote(0, 0, c, E0.at[c, :, 16:24], E0.at[c, :, 0:8], (d, t_dn)),
                remote(0, 1, c, E0.at[c, :, 8:16], E0.at[c, :, 24:32], (d, t_up)),
            )
        if kind == 1:
            return (
                remote(1, 0, c, X0.at[c, 32:40], X0.at[c, 0:8], (d_dn, t)),
                remote(1, 1, c, X0.at[c, 8:16], X0.at[c, 40:48], (d_up, t)),
            )
        if kind == 2:
            return (
                remote(2, 0, c, Y1.at[c, 32:36], Y1.at[c, 0:4], (d_dn, t)),
                remote(2, 1, c, Y1.at[c, 4:8], Y1.at[c, 36:40], (d_up, t)),
            )
        return (
            remote(3, 0, c, Z1.at[c, :, 20:24], Z1.at[c, :, 4:8], (d, t_dn)),
            remote(3, 1, c, Z1.at[c, :, 8:12], Z1.at[c, :, 24:28], (d, t_up)),
        )

    def each_present(kind, c, act, incoming=False):
        up, down = (d > 0, d < n_depth - 1) if kind in (1, 2) else (t > 0, t < n_tile - 1)
        for present, copy in zip((up, down) if incoming else (down, up), copies(kind, c)):

            @pl.when(present)
            def _():
                act(copy)

    def send(kind, c):
        each_present(kind, c, lambda copy: copy.start())

    def receive(kind, c):
        each_present(kind, c, lambda copy: copy.wait_recv(), incoming=True)

    def final_copy(c, source, target):
        return pltpu.make_async_remote_copy(
            src_ref=PT.at[c],
            dst_ref=R.at[source],
            send_sem=f_send.at[c],
            recv_sem=f_recv.at[source],
            device_id=(target, t),
            device_id_type=MESH,
        )

    def clear(cond, ref, *where):
        @pl.when(cond)
        def _():
            part = ref.at[where]
            part[...] = jnp.zeros(part.shape, jnp.float32)

    MB = 16

    def columns_smooth(buf, c, p):
        prev, cur, nxt = (
            buf[c + i, pl.ds(p, MB)].reshape(MB * NXL, W) for i in range(3)
        )
        return column_filter(prev, cur, nxt, taps[0]).reshape(MB, NXL, W)

    def load_next(field, c):
        @pl.when(c < NC - 1)
        def _():
            pltpu.make_async_copy(
                fields.at[0, :, :, 0:W], (F0, F1)[field].at[c + 2], load_sem.at[field, c + 1]
            ).wait()

    def stage_a0(c):
        load_next(0, c)

        def body(p, _):
            E0[c, pl.ds(p * MB, MB), 8:24] = columns_smooth(F0, c, p * MB)
            return 0

        lax.fori_loop(0, NZL // MB, body, 0)

    def stage_a1(c):
        load_next(1, c)

        def body(p, _):
            Y1[c, pl.ds(p * MB + 4, MB)] = columns_smooth(F1, c, p * MB)
            return 0

        lax.fori_loop(0, NZL // MB, body, 0)

    def stage_b(c):
        receive(0, c)
        clear(t == 0, E0, c, slice(None), slice(0, 8))
        clear(t == n_tile - 1, E0, c, slice(None), slice(24, 32))

        def body(p, _):
            def pairs(k):
                return E0[c, p, 4 - k : 28 - k], E0[c, p, 4 + k : 28 + k]

            X0[c, p + 8] = even_sum(E0[c, p, 4:28], pairs)
            return 0

        lax.fori_loop(0, NZL, body, 0, unroll=2)
        clear(t == 0, X0, c, slice(8, 40), slice(0, 4))
        clear(t == n_tile - 1, X0, c, slice(8, 40), slice(20, 24))
        send(1, c)

    def stage_c(c):
        receive(1, c)
        clear(d == 0, X0, c, slice(0, 8))
        clear(d == n_depth - 1, X0, c, slice(40, 48))

        def body(g, _):
            for r in range(0, 24, 8):
                planes = [X0[c, g * 8 + i, r : r + 8] for i in range(16)]
                for i in range(8):
                    S[c + 1, g * 8 + i, r : r + 8] = even_sum(
                        planes[i + 4], lambda k: (planes[i + 4 - k], planes[i + 4 + k])
                    )
            return 0

        lax.fori_loop(0, (NZL + 8) // 8, body, 0)
        clear(d == 0, S, c + 1, slice(0, 4))
        clear(d == n_depth - 1, S, c + 1, slice(36, 40))

    def stage_b1(c):
        receive(2, c)
        clear(d == 0, Y1, c, slice(0, 4))
        clear(d == n_depth - 1, Y1, c, slice(36, 40))

        def body(g, _):
            for r in range(0, 16, 8):
                planes = [Y1[c, g * 8 + i, r : r + 8] for i in range(16)]
                for i in range(8):
                    Z1[c, g * 8 + i, r + 8 : r + 16] = even_sum(
                        planes[i + 4], lambda k: (planes[i + 4 - k], planes[i + 4 + k])
                    )
            return 0

        lax.fori_loop(0, NZL // 8, body, 0)

    def gather(table, where, axis):
        return jnp.take_along_axis(table, where, axis=axis, mode="promise_in_bounds")

    G, UE = 8, 8

    def stage_d(c):
        def slope(p, _):
            prev, cur, nxt = (
                S[c + i, pl.ds(p * MB + 4, MB), 4:20].reshape(MB * NXL, W) for i in range(3)
            )
            C[c, 0, pl.ds(p * MB, MB)] = column_filter(prev, cur, nxt, taps[1]).reshape(MB, NXL, W)
            return 0

        lax.fori_loop(0, NZL // MB, slope, 0)

        def cells(p, r):
            centre = S[c + 1, p + 4, r + 4 : r + 12]
            grad_z = odd_sum(
                lambda k: (
                    S[c + 1, p + 4 - k, r + 4 : r + 12],
                    S[c + 1, p + 4 + k, r + 4 : r + 12],
                )
            )
            grad_x = odd_sum(
                lambda k: (
                    S[c + 1, p + 4, r + 4 - k : r + 12 - k],
                    S[c + 1, p + 4, r + 4 + k : r + 12 + k],
                )
            )
            grad_y = C[c, 0, p, r : r + 8]
            facing = jnp.abs(0.26726 * grad_z + 0.53452 * grad_x + 0.80178 * grad_y)
            square = grad_z * grad_z + grad_x * grad_x + grad_y * grad_y
            shade = 0.3 + 0.7 * facing * lax.rsqrt(jnp.maximum(square, LENGTH_FLOOR))
            level = 127.5 + 127.5 * jnp.tanh((0.75 * SMOOTH_SCALE) * centre)
            bin_index = jnp.minimum(level.astype(jnp.int32), 254)
            fraction = level - bin_index.astype(jnp.float32)
            pair = gather(idx[...], bin_index & 127, 1) >> ((bin_index >> 7) * 8)
            lower, upper = pair & 15, (pair >> 4) & 15
            lower_row, upper_row = lower & 7, upper & 7
            lower_half, upper_half = lower < 8, upper < 8
            found = []
            for j in range(4):
                halves = [tab[j, h] for h in range(2)]
                low, high = (
                    jnp.where(half, gather(halves[0], row, 0), gather(halves[1], row, 0))
                    for half, row in ((lower_half, lower_row), (upper_half, upper_row))
                )
                looked = low + (high - low) * fraction
                found.append(looked if j == 3 else looked * shade)
            return found

        def body(g, _):
            places = [(g * G + i, r) for i in range(G) for r in (0, 8)]
            for (p, r), found in zip(places, [cells(*place) for place in places]):
                for j in range(4):
                    C[c, j, p, r : r + 8] = found[j]
            return 0

        lax.fori_loop(0, NZL // G, body, 0)

    def stage_e(c):
        receive(3, c)
        clear(t == 0, Z1, c, slice(None), slice(4, 8))
        clear(t == n_tile - 1, Z1, c, slice(None), slice(24, 28))

        def body(p, carry):
            through, red, green, blue = carry

            def pairs(k):
                return Z1[c, p, 8 - k : 24 - k], Z1[c, p, 8 + k : 24 + k]

            smooth = even_sum(Z1[c, p, 8:24], pairs)
            gate = 0.5 + 0.5 * jnp.tanh(SMOOTH_SCALE * smooth)
            optical = (-1.5 * 2.0 / (NZL * n_depth)) * C[c, 3, p] * gate
            kept = through * jnp.exp(optical)
            weight = through - kept
            return (
                kept,
                red + weight * C[c, 0, p],
                green + weight * C[c, 1, p],
                blue + weight * C[c, 2, p],
            )

        none = jnp.zeros((NXL, W), jnp.float32)
        through, red, green, blue = lax.fori_loop(
            0, NZL, body, (jnp.ones((NXL, W), jnp.float32), none, none, none), unroll=UE
        )

        def put(ref, where):
            for j, value in enumerate((red, green, blue, through)):
                ref[where, j] = value

        @pl.when(c == d)
        def _():
            put(R, d)

        @pl.when(c != d)
        def _():
            put(PT, c)
            final_copy(c, d, c).start()

    def every(stage, start=0):
        def step(c, _):
            stage(c)
            return 0

        lax.fori_loop(start, NC, step, 0)

    taps[0] = tap_matrices(RATIO, False)
    for buf in (F0, F1):
        buf[0] = jnp.zeros_like(buf[0])
        buf[NC + 1] = jnp.zeros_like(buf[NC + 1])
    load(0, 0).wait()
    stage_a0(0)
    pl.semaphore_wait(
        barrier, n_depth - 1 + (t > 0).astype(jnp.int32) + (t < n_tile - 1).astype(jnp.int32)
    )
    send(0, 0)

    def first_field(c):
        stage_a0(c)
        send(0, c)

    every(first_field, 1)
    load(1, 0).wait()

    def second_field(c):
        stage_a1(c)
        send(2, c)

    every(second_field)
    tables()
    taps[1] = tap_matrices(SLOPE, True)
    S[0] = jnp.zeros_like(S[0])
    S[NC + 1] = jnp.zeros_like(S[NC + 1])
    every(stage_b1)

    def in_turn(j):
        return lax.rem(d + 1 + j, NC)

    def middle(i, _):
        @pl.when(i < NC)
        def _():
            stage_b(i)

        for step, turns in THIRD.items():

            @pl.when(i == step)
            def _():
                for j in turns:
                    send(3, in_turn(j))

        @pl.when((i >= 1) & (i < NC + 1))
        def _():
            stage_c(i - 1)

        @pl.when(i >= 2)
        def _():
            stage_d(i - 2)

        return 0

    lax.fori_loop(0, NC + 2, middle, 0)

    def last(j):
        stage_e(in_turn(j))

    every(last)

    def wait_final(i, _):
        @pl.when(i != d)
        def _():
            final_copy(i, i, i).wait_recv()

        return 0

    lax.fori_loop(0, n_depth, wait_final, 0)
    through, red, green, blue = R[0, 3], R[0, 0], R[0, 1], R[0, 2]
    for i in range(1, n_depth):
        red = red + through * R[i, 0]
        green = green + through * R[i, 1]
        blue = blue + through * R[i, 2]
        through = through * R[i, 3]
    for j, value in enumerate((red, green, blue, through)):
        out[j] = value

    def drain(c, _):
        for kind in range(4):
            each_present(kind, c, lambda copy: copy.wait_send())

        @pl.when(c != d)
        def _():
            final_copy(c, d, c).wait_send()

        return 0

    lax.fori_loop(0, NC, drain, 0)


def local(n_depth, n_tile, fields, colour_palette, opacity_palette, tf_index):
    _, planes, rows, columns = fields.shape
    chunks = columns // W
    f32 = jnp.float32
    vmem = pl.BlockSpec(memory_space=pltpu.VMEM)
    return pl.pallas_call(
        functools.partial(kernel, n_depth, n_tile),
        out_shape=pltpu.VMEM((4, rows, W), f32),
        in_specs=[pl.BlockSpec(memory_space=pl.ANY)] * 4,
        out_specs=vmem,
        scratch_shapes=[
            pltpu.VMEM((chunks + 2, planes, rows, W), f32),
            pltpu.VMEM((chunks + 2, planes, rows, W), f32),
            pltpu.VMEM((chunks, planes, rows + 16, W), f32),
            pltpu.VMEM((chunks, planes + 16, rows + 8, W), f32),
            pltpu.VMEM((chunks + 2, planes + 8, rows + 8, W), f32),
            pltpu.VMEM((chunks, planes + 8, rows, W), f32),
            pltpu.VMEM((chunks, planes, rows + 16, W), f32),
            pltpu.VMEM((chunks, 4, planes, rows, W), f32),
            pltpu.VMEM((chunks, 4, rows, W), f32),
            pltpu.VMEM((chunks, 4, rows, W), f32),
            pltpu.VMEM((4, 2, 8, W), f32),
            pltpu.VMEM((8, W), jnp.int32),
            pltpu.VMEM((2, 6 * W, W), jnp.bfloat16),
            pltpu.VMEM(colour_palette.shape, f32),
            pltpu.VMEM(opacity_palette.shape, f32),
            pltpu.VMEM(tf_index.shape, jnp.int32),
            pltpu.SemaphoreType.DMA((2, chunks)),
            pltpu.SemaphoreType.DMA((3,)),
            pltpu.SemaphoreType.DMA((4, 2, chunks)),
            pltpu.SemaphoreType.DMA((4, 2, chunks)),
            pltpu.SemaphoreType.DMA((chunks,)),
            pltpu.SemaphoreType.DMA((chunks,)),
        ],
        compiler_params=pltpu.CompilerParams(
            collective_id=0,
            has_side_effects=True,
            vmem_limit_bytes=56 * 1024 * 1024,
        ),
    )(fields, colour_palette, opacity_palette, tf_index)


def solution(mesh):
    placed = (P(None, "depth", "tile", None), P(), P(), P())
    return jax.shard_map(
        functools.partial(local, mesh.shape["depth"], mesh.shape["tile"]),
        mesh=mesh,
        in_specs=placed,
        out_specs=P(None, "tile", "depth"),
        check_vma=False,
    )
```

```python
import functools

import jax
import jax.numpy as jnp
import numpy as np
from jax import lax
from jax.experimental import pallas as pl
from jax.experimental.pallas import tpu as pltpu
from jax.sharding import PartitionSpec as P

MESH = pl.DeviceIdType.MESH
W = 128
THIRD = {5: (0, 1), 6: (2, 3, 4), 7: (5, 6, 7)}

offsets = np.arange(-4.0, 5.0)
bell = np.exp(-(offsets**2) / 8.0)
bell_norm = float(np.sqrt(np.sum(bell**2)))
slope_norm = float(np.sqrt(np.sum((offsets * bell) ** 2)))
RATIO = [float(np.exp(-(k * k) / 8.0)) for k in range(5)]
SMOOTH_SCALE = float(bell_norm**-3)
SLOPE = [0.0] + [float(k * RATIO[k] / RATIO[1]) for k in range(1, 5)]
SLOPE_SCALE = float(RATIO[1] / slope_norm)
LENGTH_FLOOR = float(0.1 / (SLOPE_SCALE * SMOOTH_SCALE) ** 2)


def even_sum(centre, pairs):
    total = centre
    for k in range(1, 5):
        low, high = pairs(k)
        total = total + RATIO[k] * (low + high)
    return total


def odd_sum(pairs):
    total = None
    for k in range(1, 5):
        low, high = pairs(k)
        term = high - low
        total = term if total is None else total + SLOPE[k] * term
    return total


def tap_matrices(taps, odd):
    source = lax.broadcasted_iota(jnp.int32, (W, W), 0)
    target = lax.broadcasted_iota(jnp.int32, (W, W), 1)
    halves = []
    for start in (source, jnp.where(source < 4, source + W, source - W)):
        distance = start - target
        matrix = jnp.zeros((W, W), jnp.float32)
        for k in range(-4, 5):
            tap = -taps[-k] if odd and k < 0 else taps[abs(k)]
            matrix = jnp.where(distance == k, jnp.float32(tap), matrix)
        if start is not source:
            matrix = jnp.where((source < 4) | (source >= W - 4), matrix, 0.0)
        high = matrix.astype(jnp.bfloat16)
        low = (matrix - high.astype(jnp.float32)).astype(jnp.bfloat16)
        halves += [high, high, low]
    return jnp.concatenate(halves, axis=0)


def column_filter(prev, cur, nxt, matrix):
    lane = lax.broadcasted_iota(jnp.int32, cur.shape, 1)
    pieces = []
    for values in (cur, jnp.where(lane < 4, nxt, prev)):
        high = values.astype(jnp.bfloat16)
        low = (values - high.astype(jnp.float32)).astype(jnp.bfloat16)
        pieces += [high, low, high]
    return jnp.dot(
        jnp.concatenate(pieces, axis=1), matrix, preferred_element_type=jnp.float32
    )


def kernel(
    n_depth, n_tile,
    fields, colour, opacity, entries, out,
    F0, F1, E0, X0, S, Y1, Z1, C, PT, R, tab, idx, taps, cpal, opal, tf,
    load_sem, table_sem, s_send, s_recv, f_send, f_recv,
):
    _, NZL, NXL, NYL = fields.shape
    NC = NYL // W
    d = lax.axis_index("depth")
    t = lax.axis_index("tile")
    d_up, d_dn = lax.rem(d + n_depth - 1, n_depth), lax.rem(d + 1, n_depth)
    t_up, t_dn = lax.rem(t + n_tile - 1, n_tile), lax.rem(t + 1, n_tile)

    def load(field, c):
        buf = (F0, F1)[field]
        return pltpu.make_async_copy(
            fields.at[field, :, :, c * W : (c + 1) * W], buf.at[c + 1], load_sem.at[field, c]
        )

    barrier = pltpu.get_barrier_semaphore()
    beside = ((t > 0, (d, t_up)), (t < n_tile - 1, (d, t_dn)))
    for present, where in beside:

        @pl.when(present)
        def _():
            pl.semaphore_signal(barrier, inc=1, device_id=where, device_id_type=MESH)

    for step in range(1, n_depth):
        pl.semaphore_signal(
            barrier, inc=1, device_id=(lax.rem(d + step, n_depth), t), device_id_type=MESH
        )
    for field in range(2):
        for c in range(NC):
            load(field, c).start()

    small = [
        pltpu.make_async_copy(source, target, table_sem.at[i])
        for i, (source, target) in enumerate(((colour, cpal), (opacity, opal), (entries, tf)))
    ]
    for copy in small:
        copy.start()

    def tables():
        for copy in small:
            copy.wait()
        entry = lax.broadcasted_iota(jnp.int32, (8, 16), 0)
        column = lax.broadcasted_iota(jnp.int32, (8, 16), 1)
        for j in range(4):
            row = opal[...].reshape(1, 16) if j == 3 else cpal[j : j + 1, :]
            for h in range(2):
                picked = jnp.where(column == entry + 8 * h, jnp.broadcast_to(row, (8, 16)), 0.0)
                tab[j, h] = jnp.broadcast_to(jnp.sum(picked, axis=1, keepdims=True), (8, W))
        whole = tf[...].reshape(2, W)
        low_tf = jnp.broadcast_to(whole[0:1], (8, W))
        high_tf = jnp.broadcast_to(whole[1:2], (8, W))
        lane8 = lax.broadcasted_iota(jnp.int32, (8, W), 1)
        low_next = pltpu.roll(jnp.where(lane8 >= 1, low_tf, high_tf), W - 1, 1)
        high_next = pltpu.roll(high_tf, W - 1, 1)
        idx[...] = low_tf + 16 * low_next + 256 * high_tf + 4096 * high_next

    def remote(kind, side, c, src, dst, where):
        return pltpu.make_async_remote_copy(
            src_ref=src,
            dst_ref=dst,
            send_sem=s_send.at[kind, side, c],
            recv_sem=s_recv.at[kind, side, c],
            device_id=where,
            device_id_type=MESH,
        )

    def copies(kind, c):
        if kind == 0:
            return (
                remote(0, 0, c, E0.at[c, :, 16:24], E0.at[c, :, 0:8], (d, t_dn)),
                remote(0, 1, c, E0.at[c, :, 8:16], E0.at[c, :, 24:32], (d, t_up)),
            )
        if kind == 1:
            return (
                remote(1, 0, c, X0.at[c, 32:40], X0.at[c, 0:8], (d_dn, t)),
                remote(1, 1, c, X0.at[c, 8:16], X0.at[c, 40:48], (d_up, t)),
            )
        if kind == 2:
            return (
                remote(2, 0, c, Y1.at[c, 32:36], Y1.at[c, 0:4], (d_dn, t)),
                remote(2, 1, c, Y1.at[c, 4:8], Y1.at[c, 36:40], (d_up, t)),
            )
        return (
            remote(3, 0, c, Z1.at[c, :, 20:24], Z1.at[c, :, 4:8], (d, t_dn)),
            remote(3, 1, c, Z1.at[c, :, 8:12], Z1.at[c, :, 24:28], (d, t_up)),
        )

    def each_present(kind, c, act, incoming=False):
        up, down = (d > 0, d < n_depth - 1) if kind in (1, 2) else (t > 0, t < n_tile - 1)
        for present, copy in zip((up, down) if incoming else (down, up), copies(kind, c)):

            @pl.when(present)
            def _():
                act(copy)

    def send(kind, c):
        each_present(kind, c, lambda copy: copy.start())

    def receive(kind, c):
        each_present(kind, c, lambda copy: copy.wait_recv(), incoming=True)

    def final_copy(c, source, target):
        return pltpu.make_async_remote_copy(
            src_ref=PT.at[c],
            dst_ref=R.at[source],
            send_sem=f_send.at[c],
            recv_sem=f_recv.at[source],
            device_id=(target, t),
            device_id_type=MESH,
        )

    def clear(cond, ref, *where):
        @pl.when(cond)
        def _():
            part = ref.at[where]
            part[...] = jnp.zeros(part.shape, jnp.float32)

    MB = 32

    def columns_smooth(buf, c, p):
        prev, cur, nxt = (
            buf[c + i, pl.ds(p, MB)].reshape(MB * NXL, W) for i in range(3)
        )
        return column_filter(prev, cur, nxt, taps[0]).reshape(MB, NXL, W)

    def load_next(field, c):
        @pl.when(c < NC - 1)
        def _():
            pltpu.make_async_copy(
                fields.at[0, :, :, 0:W], (F0, F1)[field].at[c + 2], load_sem.at[field, c + 1]
            ).wait()

    def stage_a0(c):
        load_next(0, c)

        def body(p, _):
            E0[c, pl.ds(p * MB, MB), 8:24] = columns_smooth(F0, c, p * MB)
            return 0

        lax.fori_loop(0, NZL // MB, body, 0)

    def stage_a1(c):
        load_next(1, c)

        def body(p, _):
            Y1[c, pl.ds(p * MB + 4, MB)] = columns_smooth(F1, c, p * MB)
            return 0

        lax.fori_loop(0, NZL // MB, body, 0)

    def stage_b(c):
        receive(0, c)
        clear(t == 0, E0, c, slice(None), slice(0, 8))
        clear(t == n_tile - 1, E0, c, slice(None), slice(24, 32))

        def body(p, _):
            def pairs(k):
                return E0[c, p, 4 - k : 28 - k], E0[c, p, 4 + k : 28 + k]

            X0[c, p + 8] = even_sum(E0[c, p, 4:28], pairs)
            return 0

        lax.fori_loop(0, NZL, body, 0, unroll=2)
        clear(t == 0, X0, c, slice(8, 40), slice(0, 4))
        clear(t == n_tile - 1, X0, c, slice(8, 40), slice(20, 24))
        send(1, c)

    def stage_c(c):
        receive(1, c)
        clear(d == 0, X0, c, slice(0, 8))
        clear(d == n_depth - 1, X0, c, slice(40, 48))

        def body(g, _):
            for r in range(0, 24, 8):
                planes = [X0[c, g * 8 + i, r : r + 8] for i in range(16)]
                for i in range(8):
                    S[c + 1, g * 8 + i, r : r + 8] = even_sum(
                        planes[i + 4], lambda k: (planes[i + 4 - k], planes[i + 4 + k])
                    )
            return 0

        lax.fori_loop(0, (NZL + 8) // 8, body, 0)
        clear(d == 0, S, c + 1, slice(0, 4))
        clear(d == n_depth - 1, S, c + 1, slice(36, 40))

    def stage_b1(c):
        receive(2, c)
        clear(d == 0, Y1, c, slice(0, 4))
        clear(d == n_depth - 1, Y1, c, slice(36, 40))

        def body(g, _):
            for r in range(0, 16, 8):
                planes = [Y1[c, g * 8 + i, r : r + 8] for i in range(16)]
                for i in range(8):
                    Z1[c, g * 8 + i, r + 8 : r + 16] = even_sum(
                        planes[i + 4], lambda k: (planes[i + 4 - k], planes[i + 4 + k])
                    )
            return 0

        lax.fori_loop(0, NZL // 8, body, 0)

    def gather(table, where, axis):
        return jnp.take_along_axis(table, where, axis=axis, mode="promise_in_bounds")

    G, UE = 8, 16

    def stage_d(c):
        def slope(p, _):
            prev, cur, nxt = (
                S[c + i, pl.ds(p * MB + 4, MB), 4:20].reshape(MB * NXL, W) for i in range(3)
            )
            C[c, 0, pl.ds(p * MB, MB)] = column_filter(prev, cur, nxt, taps[1]).reshape(MB, NXL, W)
            return 0

        lax.fori_loop(0, NZL // MB, slope, 0)

        def cells(p, r):
            centre = S[c + 1, p + 4, r + 4 : r + 12]
            grad_z = odd_sum(
                lambda k: (
                    S[c + 1, p + 4 - k, r + 4 : r + 12],
                    S[c + 1, p + 4 + k, r + 4 : r + 12],
                )
            )
            grad_x = odd_sum(
                lambda k: (
                    S[c + 1, p + 4, r + 4 - k : r + 12 - k],
                    S[c + 1, p + 4, r + 4 + k : r + 12 + k],
                )
            )
            grad_y = C[c, 0, p, r : r + 8]
            facing = jnp.abs(0.26726 * grad_z + 0.53452 * grad_x + 0.80178 * grad_y)
            square = grad_z * grad_z + grad_x * grad_x + grad_y * grad_y
            shade = 0.3 + 0.7 * facing * lax.rsqrt(jnp.maximum(square, LENGTH_FLOOR))
            level = 127.5 + 127.5 * jnp.tanh((0.75 * SMOOTH_SCALE) * centre)
            bin_index = jnp.minimum(level.astype(jnp.int32), 254)
            fraction = level - bin_index.astype(jnp.float32)
            pair = gather(idx[...], bin_index & 127, 1) >> ((bin_index >> 7) * 8)
            lower, upper = pair & 15, (pair >> 4) & 15
            lower_row, upper_row = lower & 7, upper & 7
            lower_half, upper_half = lower < 8, upper < 8
            found = []
            for j in range(4):
                halves = [tab[j, h] for h in range(2)]
                low, high = (
                    jnp.where(half, gather(halves[0], row, 0), gather(halves[1], row, 0))
                    for half, row in ((lower_half, lower_row), (upper_half, upper_row))
                )
                looked = low + (high - low) * fraction
                found.append(looked if j == 3 else looked * shade)
            return found

        def body(g, _):
            places = [(g * G + i, r) for i in range(G) for r in (0, 8)]
            for (p, r), found in zip(places, [cells(*place) for place in places]):
                for j in range(4):
                    C[c, j, p, r : r + 8] = found[j]
            return 0

        lax.fori_loop(0, NZL // G, body, 0)

    def stage_e(c):
        receive(3, c)
        clear(t == 0, Z1, c, slice(None), slice(4, 8))
        clear(t == n_tile - 1, Z1, c, slice(None), slice(24, 28))

        def body(p, carry):
            through, red, green, blue = carry

            def pairs(k):
                return Z1[c, p, 8 - k : 24 - k], Z1[c, p, 8 + k : 24 + k]

            smooth = even_sum(Z1[c, p, 8:24], pairs)
            gate = 0.5 + 0.5 * jnp.tanh(SMOOTH_SCALE * smooth)
            optical = (-1.5 * 2.0 / (NZL * n_depth)) * C[c, 3, p] * gate
            kept = through * jnp.exp(optical)
            weight = through - kept
            return (
                kept,
                red + weight * C[c, 0, p],
                green + weight * C[c, 1, p],
                blue + weight * C[c, 2, p],
            )

        none = jnp.zeros((NXL, W), jnp.float32)
        through, red, green, blue = lax.fori_loop(
            0, NZL, body, (jnp.ones((NXL, W), jnp.float32), none, none, none), unroll=UE
        )

        def put(ref, where):
            for j, value in enumerate((red, green, blue, through)):
                ref[where, j] = value

        @pl.when(c == d)
        def _():
            put(R, d)

        @pl.when(c != d)
        def _():
            put(PT, c)
            final_copy(c, d, c).start()

    def every(stage, start=0):
        def step(c, _):
            stage(c)
            return 0

        lax.fori_loop(start, NC, step, 0)

    taps[0] = tap_matrices(RATIO, False)
    for buf in (F0, F1):
        buf[0] = jnp.zeros_like(buf[0])
        buf[NC + 1] = jnp.zeros_like(buf[NC + 1])
    load(0, 0).wait()
    stage_a0(0)
    pl.semaphore_wait(
        barrier, n_depth - 1 + (t > 0).astype(jnp.int32) + (t < n_tile - 1).astype(jnp.int32)
    )
    send(0, 0)

    def first_field(c):
        stage_a0(c)
        send(0, c)

    every(first_field, 1)
    load(1, 0).wait()

    def second_field(c):
        stage_a1(c)
        send(2, c)

    every(second_field)
    tables()
    taps[1] = tap_matrices(SLOPE, True)
    S[0] = jnp.zeros_like(S[0])
    S[NC + 1] = jnp.zeros_like(S[NC + 1])
    every(stage_b1)

    def in_turn(j):
        flips = NC - 1 - j
        return sum(
            bit * lax.rem(lax.div(d, bit) + lax.div(flips, bit), 2)
            for bit in (1 << i for i in range(NC.bit_length() - 1))
        )

    def middle(i, _):
        @pl.when(i < NC)
        def _():
            stage_b(i)

        for step, turns in THIRD.items():

            @pl.when(i == step)
            def _():
                for j in turns:
                    send(3, in_turn(jnp.int32(j)))

        @pl.when((i >= 1) & (i < NC + 1))
        def _():
            stage_c(i - 1)

        @pl.when(i >= 2)
        def _():
            stage_d(i - 2)

        return 0

    lax.fori_loop(0, NC + 2, middle, 0)

    def last(j):
        stage_e(in_turn(j))

    every(last)

    def wait_final(i, _):
        @pl.when(i != d)
        def _():
            final_copy(i, i, i).wait_recv()

        return 0

    lax.fori_loop(0, n_depth, wait_final, 0)
    through, red, green, blue = R[0, 3], R[0, 0], R[0, 1], R[0, 2]
    for i in range(1, n_depth):
        red = red + through * R[i, 0]
        green = green + through * R[i, 1]
        blue = blue + through * R[i, 2]
        through = through * R[i, 3]
    for j, value in enumerate((red, green, blue, through)):
        out[j] = value

    def drain(c, _):
        for kind in range(4):
            each_present(kind, c, lambda copy: copy.wait_send())

        @pl.when(c != d)
        def _():
            final_copy(c, d, c).wait_send()

        return 0

    lax.fori_loop(0, NC, drain, 0)


def local(n_depth, n_tile, fields, colour_palette, opacity_palette, tf_index):
    _, planes, rows, columns = fields.shape
    chunks = columns // W
    f32 = jnp.float32
    vmem = pl.BlockSpec(memory_space=pltpu.VMEM)
    return pl.pallas_call(
        functools.partial(kernel, n_depth, n_tile),
        out_shape=pltpu.VMEM((4, rows, W), f32),
        in_specs=[pl.BlockSpec(memory_space=pl.ANY)] * 4,
        out_specs=vmem,
        scratch_shapes=[
            pltpu.VMEM((chunks + 2, planes, rows, W), f32),
            pltpu.VMEM((chunks + 2, planes, rows, W), f32),
            pltpu.VMEM((chunks, planes, rows + 16, W), f32),
            pltpu.VMEM((chunks, planes + 16, rows + 8, W), f32),
            pltpu.VMEM((chunks + 2, planes + 8, rows + 8, W), f32),
            pltpu.VMEM((chunks, planes + 8, rows, W), f32),
            pltpu.VMEM((chunks, planes, rows + 16, W), f32),
            pltpu.VMEM((chunks, 4, planes, rows, W), f32),
            pltpu.VMEM((chunks, 4, rows, W), f32),
            pltpu.VMEM((chunks, 4, rows, W), f32),
            pltpu.VMEM((4, 2, 8, W), f32),
            pltpu.VMEM((8, W), jnp.int32),
            pltpu.VMEM((2, 6 * W, W), jnp.bfloat16),
            pltpu.VMEM(colour_palette.shape, f32),
            pltpu.VMEM(opacity_palette.shape, f32),
            pltpu.VMEM(tf_index.shape, jnp.int32),
            pltpu.SemaphoreType.DMA((2, chunks)),
            pltpu.SemaphoreType.DMA((3,)),
            pltpu.SemaphoreType.DMA((4, 2, chunks)),
            pltpu.SemaphoreType.DMA((4, 2, chunks)),
            pltpu.SemaphoreType.DMA((chunks,)),
            pltpu.SemaphoreType.DMA((chunks,)),
        ],
        compiler_params=pltpu.CompilerParams(
            collective_id=0,
            has_side_effects=True,
            vmem_limit_bytes=56 * 1024 * 1024,
        ),
    )(fields, colour_palette, opacity_palette, tf_index)


def solution(mesh):
    placed = (P(None, "depth", "tile", None), P(), P(), P())
    return jax.shard_map(
        functools.partial(local, mesh.shape["depth"], mesh.shape["tile"]),
        mesh=mesh,
        in_specs=placed,
        out_specs=P(None, "tile", "depth"),
        check_vma=False,
    )
```

```python
import functools

import jax
import jax.numpy as jnp
import numpy as np
from jax import lax
from jax.experimental import pallas as pl
from jax.experimental.pallas import tpu as pltpu
from jax.sharding import PartitionSpec as P

MESH = pl.DeviceIdType.MESH
W = 128
THIRD = {5: (0, 1), 6: (2, 3, 4), 7: (5, 6, 7)}

offsets = np.arange(-4.0, 5.0)
bell = np.exp(-(offsets**2) / 8.0)
bell_norm = float(np.sqrt(np.sum(bell**2)))
slope_norm = float(np.sqrt(np.sum((offsets * bell) ** 2)))
RATIO = [float(np.exp(-(k * k) / 8.0)) for k in range(5)]
SMOOTH_SCALE = float(bell_norm**-3)
SLOPE = [0.0] + [float(k * RATIO[k] / RATIO[1]) for k in range(1, 5)]
SLOPE_SCALE = float(RATIO[1] / slope_norm)
LENGTH_FLOOR = float(0.1 / (SLOPE_SCALE * SMOOTH_SCALE) ** 2)


def even_sum(centre, pairs):
    total = centre
    for k in range(1, 5):
        low, high = pairs(k)
        total = total + RATIO[k] * (low + high)
    return total


def odd_sum(pairs):
    total = None
    for k in range(1, 5):
        low, high = pairs(k)
        term = high - low
        total = term if total is None else total + SLOPE[k] * term
    return total


def tap_matrices(taps, odd):
    source = lax.broadcasted_iota(jnp.int32, (W, W), 0)
    target = lax.broadcasted_iota(jnp.int32, (W, W), 1)
    halves = []
    for start in (source, jnp.where(source < 4, source + W, source - W)):
        distance = start - target
        matrix = jnp.zeros((W, W), jnp.float32)
        for k in range(-4, 5):
            tap = -taps[-k] if odd and k < 0 else taps[abs(k)]
            matrix = jnp.where(distance == k, jnp.float32(tap), matrix)
        if start is not source:
            matrix = jnp.where((source < 4) | (source >= W - 4), matrix, 0.0)
        high = matrix.astype(jnp.bfloat16)
        low = (matrix - high.astype(jnp.float32)).astype(jnp.bfloat16)
        halves += [high, high, low]
    return jnp.concatenate(halves, axis=0)


def column_filter(prev, cur, nxt, matrix):
    lane = lax.broadcasted_iota(jnp.int32, cur.shape, 1)
    pieces = []
    for values in (cur, jnp.where(lane < 4, nxt, prev)):
        high = values.astype(jnp.bfloat16)
        low = (values - high.astype(jnp.float32)).astype(jnp.bfloat16)
        pieces += [high, low, high]
    return jnp.dot(
        jnp.concatenate(pieces, axis=1), matrix, preferred_element_type=jnp.float32
    )


def kernel(
    n_depth, n_tile,
    fields, colour, opacity, entries, out,
    F0, F1, E0, X0, S, Y1, Z1, C, PT, R, tab, idx, taps, cpal, opal, tf,
    load_sem, table_sem, met_sem, s_send, s_recv, f_send, f_recv,
):
    _, NZL, NXL, NYL = fields.shape
    NC = NYL // W
    d = lax.axis_index("depth")
    t = lax.axis_index("tile")
    d_up, d_dn = lax.rem(d + n_depth - 1, n_depth), lax.rem(d + 1, n_depth)
    t_up, t_dn = lax.rem(t + n_tile - 1, n_tile), lax.rem(t + 1, n_tile)

    def load(field, c):
        buf = (F0, F1)[field]
        return pltpu.make_async_copy(
            fields.at[field, :, :, c * W : (c + 1) * W], buf.at[c + 1], load_sem.at[field, c]
        )

    barrier = pltpu.get_barrier_semaphore()
    beside = (
        (t > 0, (d, t_up)),
        (t < n_tile - 1, (d, t_dn)),
        (d > 0, (d_up, t)),
        (d < n_depth - 1, (d_dn, t)),
    )
    for present, where in beside:

        @pl.when(present)
        def _():
            pl.semaphore_signal(barrier, inc=1, device_id=where, device_id_type=MESH)

    for field in range(2):
        for c in range(NC):
            load(field, c).start()

    small = [
        pltpu.make_async_copy(source, target, table_sem.at[i])
        for i, (source, target) in enumerate(((colour, cpal), (opacity, opal), (entries, tf)))
    ]
    for copy in small:
        copy.start()

    to_power = float(-0.5 * 1.5 * 2.0 / (NZL * n_depth) / np.log(2.0))

    def tables():
        for copy in small:
            copy.wait()
        entry = lax.broadcasted_iota(jnp.int32, (8, 16), 0)
        column = lax.broadcasted_iota(jnp.int32, (8, 16), 1)
        for j in range(4):
            row = cpal[j : j + 1, :] if j < 3 else opal[...].reshape(1, 16) * to_power
            for h in range(2):
                picked = jnp.where(column == entry + 8 * h, jnp.broadcast_to(row, (8, 16)), 0.0)
                tab[j, h] = jnp.broadcast_to(jnp.sum(picked, axis=1, keepdims=True), (8, W))
        whole = tf[...].reshape(2, W)
        low_tf = jnp.broadcast_to(whole[0:1], (8, W))
        high_tf = jnp.broadcast_to(whole[1:2], (8, W))
        lane8 = lax.broadcasted_iota(jnp.int32, (8, W), 1)
        low_next = pltpu.roll(jnp.where(lane8 >= 1, low_tf, high_tf), W - 1, 1)
        high_next = pltpu.roll(high_tf, W - 1, 1)
        idx[...] = low_tf + 16 * low_next + 256 * high_tf + 4096 * high_next

    def remote(kind, side, c, src, dst, where):
        return pltpu.make_async_remote_copy(
            src_ref=src,
            dst_ref=dst,
            send_sem=s_send.at[kind, side, c],
            recv_sem=s_recv.at[kind, side, c],
            device_id=where,
            device_id_type=MESH,
        )

    def copies(kind, c):
        if kind == 0:
            return (
                remote(0, 0, c, E0.at[c, :, 16:24], E0.at[c, :, 0:8], (d, t_dn)),
                remote(0, 1, c, E0.at[c, :, 8:16], E0.at[c, :, 24:32], (d, t_up)),
            )
        if kind == 1:
            return (
                remote(1, 0, c, X0.at[c, 32:40], X0.at[c, 0:8], (d_dn, t)),
                remote(1, 1, c, X0.at[c, 8:16], X0.at[c, 40:48], (d_up, t)),
            )
        if kind == 2:
            return (
                remote(2, 0, c, Y1.at[c, 32:36], Y1.at[c, 0:4], (d_dn, t)),
                remote(2, 1, c, Y1.at[c, 4:8], Y1.at[c, 36:40], (d_up, t)),
            )
        return (
            remote(3, 0, c, Z1.at[c, :, 20:24], Z1.at[c, :, 4:8], (d, t_dn)),
            remote(3, 1, c, Z1.at[c, :, 8:12], Z1.at[c, :, 24:28], (d, t_up)),
        )

    def each_present(kind, c, act, incoming=False):
        up, down = (d > 0, d < n_depth - 1) if kind in (1, 2) else (t > 0, t < n_tile - 1)
        for present, copy in zip((up, down) if incoming else (down, up), copies(kind, c)):

            @pl.when(present)
            def _():
                act(copy)

    def send(kind, c):
        each_present(kind, c, lambda copy: copy.start())

    def receive(kind, c):
        each_present(kind, c, lambda copy: copy.wait_recv(), incoming=True)

    def final_copy(c, source, target):
        return pltpu.make_async_remote_copy(
            src_ref=PT.at[c],
            dst_ref=R.at[source],
            send_sem=f_send.at[c],
            recv_sem=f_recv.at[source],
            device_id=(target, t),
            device_id_type=MESH,
        )

    def clear(cond, ref, *where):
        @pl.when(cond)
        def _():
            part = ref.at[where]
            part[...] = jnp.zeros(part.shape, jnp.float32)

    MB = 32

    def columns_smooth(buf, c, p):
        prev, cur, nxt = (
            buf[c + i, pl.ds(p, MB)].reshape(MB * NXL, W) for i in range(3)
        )
        return column_filter(prev, cur, nxt, taps[0]).reshape(MB, NXL, W)

    def load_next(field, c):
        @pl.when(c < NC - 1)
        def _():
            pltpu.make_async_copy(
                fields.at[0, :, :, 0:W], (F0, F1)[field].at[c + 2], load_sem.at[field, c + 1]
            ).wait()

    def stage_a0(c):
        load_next(0, c)

        def body(p, _):
            E0[c, pl.ds(p * MB, MB), 8:24] = columns_smooth(F0, c, p * MB)
            return 0

        lax.fori_loop(0, NZL // MB, body, 0)

    def stage_a1(c):
        load_next(1, c)

        def body(p, _):
            Y1[c, pl.ds(p * MB + 4, MB)] = columns_smooth(F1, c, p * MB)
            return 0

        lax.fori_loop(0, NZL // MB, body, 0)

    def stage_b(c):
        receive(0, c)
        clear(t == 0, E0, c, slice(None), slice(0, 8))
        clear(t == n_tile - 1, E0, c, slice(None), slice(24, 32))

        def body(p, _):
            def pairs(k):
                return E0[c, p, 4 - k : 28 - k], E0[c, p, 4 + k : 28 + k]

            X0[c, p + 8] = even_sum(E0[c, p, 4:28], pairs)
            return 0

        lax.fori_loop(0, NZL, body, 0, unroll=2)
        clear(t == 0, X0, c, slice(8, 40), slice(0, 4))
        clear(t == n_tile - 1, X0, c, slice(8, 40), slice(20, 24))
        send(1, c)

    def stage_c(c):
        receive(1, c)
        clear(d == 0, X0, c, slice(0, 8))
        clear(d == n_depth - 1, X0, c, slice(40, 48))

        def body(g, _):
            for r in range(0, 24, 8):
                planes = [X0[c, g * 8 + i, r : r + 8] for i in range(16)]
                for i in range(8):
                    S[c + 1, g * 8 + i, r : r + 8] = even_sum(
                        planes[i + 4], lambda k: (planes[i + 4 - k], planes[i + 4 + k])
                    )
            return 0

        lax.fori_loop(0, (NZL + 8) // 8, body, 0)
        clear(d == 0, S, c + 1, slice(0, 4))
        clear(d == n_depth - 1, S, c + 1, slice(36, 40))

    def stage_b1(c):
        receive(2, c)
        clear(d == 0, Y1, c, slice(0, 4))
        clear(d == n_depth - 1, Y1, c, slice(36, 40))

        def body(g, _):
            for r in range(0, 16, 8):
                planes = [Y1[c, g * 8 + i, r : r + 8] for i in range(16)]
                for i in range(8):
                    Z1[c, g * 8 + i, r + 8 : r + 16] = even_sum(
                        planes[i + 4], lambda k: (planes[i + 4 - k], planes[i + 4 + k])
                    )
            return 0

        lax.fori_loop(0, NZL // 8, body, 0)

    def gather(table, where, axis):
        return jnp.take_along_axis(table, where, axis=axis, mode="promise_in_bounds")

    G, UE = 8, 16

    def stage_d(c):
        def slope(p, _):
            prev, cur, nxt = (
                S[c + i, pl.ds(p * MB + 4, MB), 4:20].reshape(MB * NXL, W) for i in range(3)
            )
            C[c, 0, pl.ds(p * MB, MB)] = column_filter(prev, cur, nxt, taps[1]).reshape(MB, NXL, W)
            return 0

        lax.fori_loop(0, NZL // MB, slope, 0)

        def cells(p, r):
            centre = S[c + 1, p + 4, r + 4 : r + 12]
            grad_z = odd_sum(
                lambda k: (
                    S[c + 1, p + 4 - k, r + 4 : r + 12],
                    S[c + 1, p + 4 + k, r + 4 : r + 12],
                )
            )
            grad_x = odd_sum(
                lambda k: (
                    S[c + 1, p + 4, r + 4 - k : r + 12 - k],
                    S[c + 1, p + 4, r + 4 + k : r + 12 + k],
                )
            )
            grad_y = C[c, 0, p, r : r + 8]
            facing = jnp.abs(0.26726 * grad_z + 0.53452 * grad_x + 0.80178 * grad_y)
            square = grad_z * grad_z + grad_x * grad_x + grad_y * grad_y
            shade = 0.3 + 0.7 * facing * lax.rsqrt(jnp.maximum(square, LENGTH_FLOOR))
            level = 127.5 + 127.5 * jnp.tanh((0.75 * SMOOTH_SCALE) * centre)
            bin_index = jnp.minimum(level.astype(jnp.int32), 254)
            fraction = level - bin_index.astype(jnp.float32)
            pair = gather(idx[...], bin_index & 127, 1) >> ((bin_index >> 7) * 8)
            lower, upper = pair & 15, (pair >> 4) & 15
            lower_row, upper_row = lower & 7, upper & 7
            lower_half, upper_half = lower < 8, upper < 8
            found = []
            for j in range(4):
                halves = [tab[j, h] for h in range(2)]
                low, high = (
                    jnp.where(half, gather(halves[0], row, 0), gather(halves[1], row, 0))
                    for half, row in ((lower_half, lower_row), (upper_half, upper_row))
                )
                looked = low + (high - low) * fraction
                found.append(looked if j == 3 else looked * shade)
            return found

        def body(g, _):
            places = [(g * G + i, r) for i in range(G) for r in (0, 8)]
            for (p, r), found in zip(places, [cells(*place) for place in places]):
                for j in range(4):
                    C[c, j, p, r : r + 8] = found[j]
            return 0

        lax.fori_loop(0, NZL // G, body, 0)

    def stage_e(c):
        receive(3, c)
        clear(t == 0, Z1, c, slice(None), slice(4, 8))
        clear(t == n_tile - 1, Z1, c, slice(None), slice(24, 28))

        def body(p, carry):
            through, red, green, blue = carry

            def pairs(k):
                return Z1[c, p, 8 - k : 24 - k], Z1[c, p, 8 + k : 24 + k]

            smooth = even_sum(Z1[c, p, 8:24], pairs)
            most = C[c, 3, p]
            kept = through * jnp.exp2(most + most * jnp.tanh(SMOOTH_SCALE * smooth))
            weight = through - kept
            return (
                kept,
                red + weight * C[c, 0, p],
                green + weight * C[c, 1, p],
                blue + weight * C[c, 2, p],
            )

        none = jnp.zeros((NXL, W), jnp.float32)
        through, red, green, blue = lax.fori_loop(
            0, NZL, body, (jnp.ones((NXL, W), jnp.float32), none, none, none), unroll=UE
        )

        def put(ref, where):
            for j, value in enumerate((red, green, blue, through)):
                ref[where, j] = value

        @pl.when(c == d)
        def _():
            put(R, d)

        @pl.when(c != d)
        def _():
            put(PT, c)
            final_copy(c, d, c).start()

    def greetings(r):
        return (
            (d >= 2**r, lax.rem(d + n_depth - 2**r, n_depth), 1),
            (d < n_depth - 2**r, lax.rem(d + 2**r, n_depth), 0),
        )

    def greet(r):
        for present, where, side in greetings(r):

            @pl.when(present)
            def _():
                pl.semaphore_signal(
                    met_sem.at[r, side], inc=1, device_id=(where, t), device_id_type=MESH
                )

    def met(r):
        for present, _, side in greetings(r):

            @pl.when(present)
            def _():
                pl.semaphore_wait(met_sem.at[r, 1 - side], 1)

    def every(stage, start=0):
        def step(c, _):
            stage(c)
            return 0

        lax.fori_loop(start, NC, step, 0)

    taps[0] = tap_matrices(RATIO, False)
    for buf in (F0, F1):
        buf[0] = jnp.zeros_like(buf[0])
        buf[NC + 1] = jnp.zeros_like(buf[NC + 1])
    load(0, 0).wait()
    stage_a0(0)
    pl.semaphore_wait(barrier, sum(present.astype(jnp.int32) for present, _ in beside))
    send(0, 0)
    greet(0)

    def first_field(c):
        stage_a0(c)
        send(0, c)

    every(first_field, 1)
    met(0)
    greet(1)
    load(1, 0).wait()

    def second_field(c):
        stage_a1(c)
        send(2, c)

    every(second_field)
    met(1)
    greet(2)
    tables()
    taps[1] = tap_matrices(SLOPE, True)
    S[0] = jnp.zeros_like(S[0])
    S[NC + 1] = jnp.zeros_like(S[NC + 1])
    every(stage_b1)

    def in_turn(j):
        flips = NC - 1 - j
        return sum(
            bit * lax.rem(lax.div(d, bit) + lax.div(flips, bit), 2)
            for bit in (1 << i for i in range(NC.bit_length() - 1))
        )

    def middle(i, _):
        @pl.when(i < NC)
        def _():
            stage_b(i)

        for step, turns in THIRD.items():

            @pl.when(i == step)
            def _():
                for j in turns:
                    send(3, in_turn(jnp.int32(j)))

        @pl.when((i >= 1) & (i < NC + 1))
        def _():
            stage_c(i - 1)

        @pl.when(i >= 2)
        def _():
            stage_d(i - 2)

        return 0

    lax.fori_loop(0, NC + 2, middle, 0)

    def last(j):
        stage_e(in_turn(j))

    met(2)
    every(last)

    def wait_final(i, _):
        @pl.when(i != d)
        def _():
            final_copy(i, i, i).wait_recv()

        return 0

    lax.fori_loop(0, n_depth, wait_final, 0)
    through, red, green, blue = R[0, 3], R[0, 0], R[0, 1], R[0, 2]
    for i in range(1, n_depth):
        red = red + through * R[i, 0]
        green = green + through * R[i, 1]
        blue = blue + through * R[i, 2]
        through = through * R[i, 3]
    for j, value in enumerate((red, green, blue, through)):
        out[j] = value

    def drain(c, _):
        for kind in range(4):
            each_present(kind, c, lambda copy: copy.wait_send())

        @pl.when(c != d)
        def _():
            final_copy(c, d, c).wait_send()

        return 0

    lax.fori_loop(0, NC, drain, 0)


def local(n_depth, n_tile, fields, colour_palette, opacity_palette, tf_index):
    _, planes, rows, columns = fields.shape
    chunks = columns // W
    f32 = jnp.float32
    vmem = pl.BlockSpec(memory_space=pltpu.VMEM)
    return pl.pallas_call(
        functools.partial(kernel, n_depth, n_tile),
        out_shape=pltpu.VMEM((4, rows, W), f32),
        in_specs=[pl.BlockSpec(memory_space=pl.ANY)] * 4,
        out_specs=vmem,
        scratch_shapes=[
            pltpu.VMEM((chunks + 2, planes, rows, W), f32),
            pltpu.VMEM((chunks + 2, planes, rows, W), f32),
            pltpu.VMEM((chunks, planes, rows + 16, W), f32),
            pltpu.VMEM((chunks, planes + 16, rows + 8, W), f32),
            pltpu.VMEM((chunks + 2, planes + 8, rows + 8, W), f32),
            pltpu.VMEM((chunks, planes + 8, rows, W), f32),
            pltpu.VMEM((chunks, planes, rows + 16, W), f32),
            pltpu.VMEM((chunks, 4, planes, rows, W), f32),
            pltpu.VMEM((chunks, 4, rows, W), f32),
            pltpu.VMEM((chunks, 4, rows, W), f32),
            pltpu.VMEM((4, 2, 8, W), f32),
            pltpu.VMEM((8, W), jnp.int32),
            pltpu.VMEM((2, 6 * W, W), jnp.bfloat16),
            pltpu.VMEM(colour_palette.shape, f32),
            pltpu.VMEM(opacity_palette.shape, f32),
            pltpu.VMEM(tf_index.shape, jnp.int32),
            pltpu.SemaphoreType.DMA((2, chunks)),
            pltpu.SemaphoreType.DMA((3,)),
            pltpu.SemaphoreType.REGULAR((3, 2)),
            pltpu.SemaphoreType.DMA((4, 2, chunks)),
            pltpu.SemaphoreType.DMA((4, 2, chunks)),
            pltpu.SemaphoreType.DMA((chunks,)),
            pltpu.SemaphoreType.DMA((chunks,)),
        ],
        compiler_params=pltpu.CompilerParams(
            collective_id=0,
            has_side_effects=True,
            vmem_limit_bytes=56 * 1024 * 1024,
        ),
    )(fields, colour_palette, opacity_palette, tf_index)


def solution(mesh):
    placed = (P(None, "depth", "tile", None), P(), P(), P())
    return jax.shard_map(
        functools.partial(local, mesh.shape["depth"], mesh.shape["tile"]),
        mesh=mesh,
        in_specs=placed,
        out_specs=P(None, "tile", "depth"),
        check_vma=False,
    )
```

```python
import functools

import jax
import jax.numpy as jnp
import numpy as np
from jax import lax
from jax.experimental import pallas as pl
from jax.experimental.pallas import tpu as pltpu
from jax.sharding import PartitionSpec as P

MESH = pl.DeviceIdType.MESH
W = 128
THIRD = {0: tuple(range(8))}

offsets = np.arange(-4.0, 5.0)
bell = np.exp(-(offsets**2) / 8.0)
bell_norm = float(np.sqrt(np.sum(bell**2)))
slope_norm = float(np.sqrt(np.sum((offsets * bell) ** 2)))
RATIO = [float(np.exp(-(k * k) / 8.0)) for k in range(5)]
SMOOTH_SCALE = float(bell_norm**-3)
SLOPE = [0.0] + [float(k * RATIO[k] / RATIO[1]) for k in range(1, 5)]
SLOPE_SCALE = float(RATIO[1] / slope_norm)
LENGTH_FLOOR = float(0.1 / (SLOPE_SCALE * SMOOTH_SCALE) ** 2)


def even_sum(centre, pairs):
    total = centre
    for k in range(1, 5):
        low, high = pairs(k)
        total = total + RATIO[k] * (low + high)
    return total


def odd_sum(pairs):
    total = None
    for k in range(1, 5):
        low, high = pairs(k)
        term = high - low
        total = term if total is None else total + SLOPE[k] * term
    return total


def tap_matrices(taps, odd):
    source = lax.broadcasted_iota(jnp.int32, (W, W), 0)
    target = lax.broadcasted_iota(jnp.int32, (W, W), 1)
    halves = []
    for start in (source, jnp.where(source < 4, source + W, source - W)):
        distance = start - target
        matrix = jnp.zeros((W, W), jnp.float32)
        for k in range(-4, 5):
            tap = -taps[-k] if odd and k < 0 else taps[abs(k)]
            matrix = jnp.where(distance == k, jnp.float32(tap), matrix)
        if start is not source:
            matrix = jnp.where((source < 4) | (source >= W - 4), matrix, 0.0)
        high = matrix.astype(jnp.bfloat16)
        low = (matrix - high.astype(jnp.float32)).astype(jnp.bfloat16)
        halves += [high, high, low]
    return jnp.concatenate(halves, axis=0)


def column_filter(prev, cur, nxt, matrix):
    lane = lax.broadcasted_iota(jnp.int32, cur.shape, 1)
    pieces = []
    for values in (cur, jnp.where(lane < 4, nxt, prev)):
        high = values.astype(jnp.bfloat16)
        low = (values - high.astype(jnp.float32)).astype(jnp.bfloat16)
        pieces += [high, low, high]
    return jnp.dot(
        jnp.concatenate(pieces, axis=1), matrix, preferred_element_type=jnp.float32
    )


def kernel(
    n_depth, n_tile,
    fields, colour, opacity, entries, out,
    F0, F1, E0, X0, S, Y1, Z1, C, PT, R, tab, idx, taps, cpal, opal, tf,
    load_sem, table_sem, met_sem, s_send, s_recv, f_send, f_recv,
):
    _, NZL, NXL, NYL = fields.shape
    NC = NYL // W
    d = lax.axis_index("depth")
    t = lax.axis_index("tile")
    d_up, d_dn = lax.rem(d + n_depth - 1, n_depth), lax.rem(d + 1, n_depth)
    t_up, t_dn = lax.rem(t + n_tile - 1, n_tile), lax.rem(t + 1, n_tile)

    def load(field, c):
        buf = (F0, F1)[field]
        return pltpu.make_async_copy(
            fields.at[field, :, :, c * W : (c + 1) * W], buf.at[c + 1], load_sem.at[field, c]
        )

    barrier = pltpu.get_barrier_semaphore()
    beside = (
        (t > 0, (d, t_up)),
        (t < n_tile - 1, (d, t_dn)),
        (d > 0, (d_up, t)),
        (d < n_depth - 1, (d_dn, t)),
    )
    for present, where in beside:

        @pl.when(present)
        def _():
            pl.semaphore_signal(barrier, inc=1, device_id=where, device_id_type=MESH)

    for field in range(2):
        for c in range(NC):
            load(field, c).start()

    small = [
        pltpu.make_async_copy(source, target, table_sem.at[i])
        for i, (source, target) in enumerate(((colour, cpal), (opacity, opal), (entries, tf)))
    ]
    for copy in small:
        copy.start()

    to_power = float(-0.5 * 1.5 * 2.0 / (NZL * n_depth) / np.log(2.0))

    def tables():
        for copy in small:
            copy.wait()
        entry = lax.broadcasted_iota(jnp.int32, (8, 16), 0)
        column = lax.broadcasted_iota(jnp.int32, (8, 16), 1)
        for j in range(4):
            row = cpal[j : j + 1, :] if j < 3 else opal[...].reshape(1, 16) * to_power
            for h in range(2):
                picked = jnp.where(column == entry + 8 * h, jnp.broadcast_to(row, (8, 16)), 0.0)
                tab[j, h] = jnp.broadcast_to(jnp.sum(picked, axis=1, keepdims=True), (8, W))
        whole = tf[...].reshape(2, W)
        low_tf = jnp.broadcast_to(whole[0:1], (8, W))
        high_tf = jnp.broadcast_to(whole[1:2], (8, W))
        lane8 = lax.broadcasted_iota(jnp.int32, (8, W), 1)
        low_next = pltpu.roll(jnp.where(lane8 >= 1, low_tf, high_tf), W - 1, 1)
        high_next = pltpu.roll(high_tf, W - 1, 1)
        idx[...] = low_tf + 16 * low_next + 256 * high_tf + 4096 * high_next

    def remote(kind, side, c, src, dst, where):
        return pltpu.make_async_remote_copy(
            src_ref=src,
            dst_ref=dst,
            send_sem=s_send.at[kind, side, c],
            recv_sem=s_recv.at[kind, side, c],
            device_id=where,
            device_id_type=MESH,
        )

    def copies(kind, c):
        if kind == 0:
            return (
                remote(0, 0, c, E0.at[c, :, 16:24], E0.at[c, :, 0:8], (d, t_dn)),
                remote(0, 1, c, E0.at[c, :, 8:16], E0.at[c, :, 24:32], (d, t_up)),
            )
        if kind == 1:
            return (
                remote(1, 0, c, X0.at[c, 32:40], X0.at[c, 0:8], (d_dn, t)),
                remote(1, 1, c, X0.at[c, 8:16], X0.at[c, 40:48], (d_up, t)),
            )
        if kind == 2:
            return (
                remote(2, 0, c, Y1.at[c, 32:36], Y1.at[c, 0:4], (d_dn, t)),
                remote(2, 1, c, Y1.at[c, 4:8], Y1.at[c, 36:40], (d_up, t)),
            )
        return (
            remote(3, 0, c, Z1.at[c, :, 20:24], Z1.at[c, :, 4:8], (d, t_dn)),
            remote(3, 1, c, Z1.at[c, :, 8:12], Z1.at[c, :, 24:28], (d, t_up)),
        )

    def each_present(kind, c, act, incoming=False):
        up, down = (d > 0, d < n_depth - 1) if kind in (1, 2) else (t > 0, t < n_tile - 1)
        for present, copy in zip((up, down) if incoming else (down, up), copies(kind, c)):

            @pl.when(present)
            def _():
                act(copy)

    def send(kind, c):
        each_present(kind, c, lambda copy: copy.start())

    def receive(kind, c):
        each_present(kind, c, lambda copy: copy.wait_recv(), incoming=True)

    def final_copy(c, source, target):
        return pltpu.make_async_remote_copy(
            src_ref=PT.at[c],
            dst_ref=R.at[source],
            send_sem=f_send.at[c],
            recv_sem=f_recv.at[source],
            device_id=(target, t),
            device_id_type=MESH,
        )

    def clear(cond, ref, *where):
        @pl.when(cond)
        def _():
            part = ref.at[where]
            part[...] = jnp.zeros(part.shape, jnp.float32)

    MB = 32

    def columns_smooth(buf, c, p):
        prev, cur, nxt = (
            buf[c + i, pl.ds(p, MB)].reshape(MB * NXL, W) for i in range(3)
        )
        return column_filter(prev, cur, nxt, taps[0]).reshape(MB, NXL, W)

    def load_next(field, c):
        @pl.when(c < NC - 1)
        def _():
            pltpu.make_async_copy(
                fields.at[0, :, :, 0:W], (F0, F1)[field].at[c + 2], load_sem.at[field, c + 1]
            ).wait()

    def stage_a0(c):
        load_next(0, c)

        def body(p, _):
            E0[c, pl.ds(p * MB, MB), 8:24] = columns_smooth(F0, c, p * MB)
            return 0

        lax.fori_loop(0, NZL // MB, body, 0)

    def stage_a1(c):
        load_next(1, c)

        def body(p, _):
            Y1[c, pl.ds(p * MB + 4, MB)] = columns_smooth(F1, c, p * MB)
            return 0

        lax.fori_loop(0, NZL // MB, body, 0)

    def stage_b(c):
        receive(0, c)
        clear(t == 0, E0, c, slice(None), slice(0, 8))
        clear(t == n_tile - 1, E0, c, slice(None), slice(24, 32))

        def body(p, _):
            def pairs(k):
                return E0[c, p, 4 - k : 28 - k], E0[c, p, 4 + k : 28 + k]

            X0[c, p + 8] = even_sum(E0[c, p, 4:28], pairs)
            return 0

        lax.fori_loop(0, NZL, body, 0, unroll=2)
        clear(t == 0, X0, c, slice(8, 40), slice(0, 4))
        clear(t == n_tile - 1, X0, c, slice(8, 40), slice(20, 24))
        send(1, c)

    def stage_c(c):
        receive(1, c)
        clear(d == 0, X0, c, slice(0, 8))
        clear(d == n_depth - 1, X0, c, slice(40, 48))

        def body(g, _):
            for r in range(0, 24, 8):
                planes = [X0[c, g * 8 + i, r : r + 8] for i in range(16)]
                for i in range(8):
                    S[c + 1, g * 8 + i, r : r + 8] = even_sum(
                        planes[i + 4], lambda k: (planes[i + 4 - k], planes[i + 4 + k])
                    )
            return 0

        lax.fori_loop(0, (NZL + 8) // 8, body, 0)
        clear(d == 0, S, c + 1, slice(0, 4))
        clear(d == n_depth - 1, S, c + 1, slice(36, 40))

    def stage_b1(c):
        receive(2, c)
        clear(d == 0, Y1, c, slice(0, 4))
        clear(d == n_depth - 1, Y1, c, slice(36, 40))

        def body(g, _):
            for r in range(0, 16, 8):
                planes = [Y1[c, g * 8 + i, r : r + 8] for i in range(16)]
                for i in range(8):
                    Z1[c, g * 8 + i, r + 8 : r + 16] = even_sum(
                        planes[i + 4], lambda k: (planes[i + 4 - k], planes[i + 4 + k])
                    )
            return 0

        lax.fori_loop(0, NZL // 8, body, 0)

    def gather(table, where, axis):
        return jnp.take_along_axis(table, where, axis=axis, mode="promise_in_bounds")

    G, UE = 8, 16

    def stage_d(c):
        def slope(p, _):
            prev, cur, nxt = (
                S[c + i, pl.ds(p * MB + 4, MB), 4:20].reshape(MB * NXL, W) for i in range(3)
            )
            C[c, 0, pl.ds(p * MB, MB)] = column_filter(prev, cur, nxt, taps[1]).reshape(MB, NXL, W)
            return 0

        lax.fori_loop(0, NZL // MB, slope, 0)

        def cells(p, r):
            centre = S[c + 1, p + 4, r + 4 : r + 12]
            grad_z = odd_sum(
                lambda k: (
                    S[c + 1, p + 4 - k, r + 4 : r + 12],
                    S[c + 1, p + 4 + k, r + 4 : r + 12],
                )
            )
            grad_x = odd_sum(
                lambda k: (
                    S[c + 1, p + 4, r + 4 - k : r + 12 - k],
                    S[c + 1, p + 4, r + 4 + k : r + 12 + k],
                )
            )
            grad_y = C[c, 0, p, r : r + 8]
            facing = jnp.abs(0.26726 * grad_z + 0.53452 * grad_x + 0.80178 * grad_y)
            square = grad_z * grad_z + grad_x * grad_x + grad_y * grad_y
            shade = 0.3 + 0.7 * facing * lax.rsqrt(jnp.maximum(square, LENGTH_FLOOR))
            level = 127.5 + 127.5 * jnp.tanh((0.75 * SMOOTH_SCALE) * centre)
            bin_index = jnp.minimum(level.astype(jnp.int32), 254)
            fraction = level - bin_index.astype(jnp.float32)
            pair = gather(idx[...], bin_index & 127, 1) >> ((bin_index >> 7) * 8)
            lower, upper = pair & 15, (pair >> 4) & 15
            lower_row, upper_row = lower & 7, upper & 7
            lower_half, upper_half = lower < 8, upper < 8
            found = []
            for j in range(4):
                halves = [tab[j, h] for h in range(2)]
                low, high = (
                    jnp.where(half, gather(halves[0], row, 0), gather(halves[1], row, 0))
                    for half, row in ((lower_half, lower_row), (upper_half, upper_row))
                )
                looked = low + (high - low) * fraction
                found.append(looked if j == 3 else looked * shade)
            return found

        def body(g, _):
            places = [(g * G + i, r) for i in range(G) for r in (0, 8)]
            for (p, r), found in zip(places, [cells(*place) for place in places]):
                for j in range(4):
                    C[c, j, p, r : r + 8] = found[j]
            return 0

        lax.fori_loop(0, NZL // G, body, 0)

    def stage_e(c):
        receive(3, c)
        clear(t == 0, Z1, c, slice(None), slice(4, 8))
        clear(t == n_tile - 1, Z1, c, slice(None), slice(24, 28))

        def body(p, carry):
            through, red, green, blue = carry

            def pairs(k):
                return Z1[c, p, 8 - k : 24 - k], Z1[c, p, 8 + k : 24 + k]

            smooth = even_sum(Z1[c, p, 8:24], pairs)
            most = C[c, 3, p]
            kept = through * jnp.exp2(most + most * jnp.tanh(SMOOTH_SCALE * smooth))
            weight = through - kept
            return (
                kept,
                red + weight * C[c, 0, p],
                green + weight * C[c, 1, p],
                blue + weight * C[c, 2, p],
            )

        none = jnp.zeros((NXL, W), jnp.float32)
        through, red, green, blue = lax.fori_loop(
            0, NZL, body, (jnp.ones((NXL, W), jnp.float32), none, none, none), unroll=UE
        )

        def put(ref, where):
            for j, value in enumerate((red, green, blue, through)):
                ref[where, j] = value

        @pl.when(c == d)
        def _():
            put(R, d)

        @pl.when(c != d)
        def _():
            put(PT, c)
            final_copy(c, d, c).start()

    def greetings(r):
        return (
            (d >= 2**r, lax.rem(d + n_depth - 2**r, n_depth), 1),
            (d < n_depth - 2**r, lax.rem(d + 2**r, n_depth), 0),
        )

    def greet(r):
        for present, where, side in greetings(r):

            @pl.when(present)
            def _():
                pl.semaphore_signal(
                    met_sem.at[r, side], inc=1, device_id=(where, t), device_id_type=MESH
                )

    def met(r):
        for present, _, side in greetings(r):

            @pl.when(present)
            def _():
                pl.semaphore_wait(met_sem.at[r, 1 - side], 1)

    def every(stage, start=0):
        def step(c, _):
            stage(c)
            return 0

        lax.fori_loop(start, NC, step, 0)

    taps[0] = tap_matrices(RATIO, False)
    for buf in (F0, F1):
        buf[0] = jnp.zeros_like(buf[0])
        buf[NC + 1] = jnp.zeros_like(buf[NC + 1])
    load(0, 0).wait()
    stage_a0(0)
    pl.semaphore_wait(barrier, sum(present.astype(jnp.int32) for present, _ in beside))
    send(0, 0)
    greet(0)

    def first_field(c):
        stage_a0(c)
        send(0, c)

    every(first_field, 1)
    met(0)
    greet(1)
    load(1, 0).wait()

    def second_field(c):
        stage_a1(c)
        send(2, c)

    every(second_field)
    met(1)
    greet(2)
    tables()
    taps[1] = tap_matrices(SLOPE, True)
    S[0] = jnp.zeros_like(S[0])
    S[NC + 1] = jnp.zeros_like(S[NC + 1])
    every(stage_b1)

    def in_turn(j):
        flips = NC - 1 - j
        return sum(
            bit * lax.rem(lax.div(d, bit) + lax.div(flips, bit), 2)
            for bit in (1 << i for i in range(NC.bit_length() - 1))
        )

    def middle(i, _):
        @pl.when(i < NC)
        def _():
            stage_b(i)

        for step, turns in THIRD.items():

            @pl.when(i == step)
            def _():
                for j in turns:
                    send(3, in_turn(jnp.int32(j)))

        @pl.when((i >= 1) & (i < NC + 1))
        def _():
            stage_c(i - 1)

        @pl.when(i >= 2)
        def _():
            stage_d(i - 2)

        return 0

    lax.fori_loop(0, NC + 2, middle, 0)

    def last(j):
        stage_e(in_turn(j))

    met(2)
    every(last)

    def wait_final(i, _):
        @pl.when(i != d)
        def _():
            final_copy(i, i, i).wait_recv()

        return 0

    lax.fori_loop(0, n_depth, wait_final, 0)
    through, red, green, blue = R[0, 3], R[0, 0], R[0, 1], R[0, 2]
    for i in range(1, n_depth):
        red = red + through * R[i, 0]
        green = green + through * R[i, 1]
        blue = blue + through * R[i, 2]
        through = through * R[i, 3]
    for j, value in enumerate((red, green, blue, through)):
        out[j] = value

    def drain(c, _):
        for kind in range(4):
            each_present(kind, c, lambda copy: copy.wait_send())

        @pl.when(c != d)
        def _():
            final_copy(c, d, c).wait_send()

        return 0

    lax.fori_loop(0, NC, drain, 0)


def local(n_depth, n_tile, fields, colour_palette, opacity_palette, tf_index):
    _, planes, rows, columns = fields.shape
    chunks = columns // W
    f32 = jnp.float32
    vmem = pl.BlockSpec(memory_space=pltpu.VMEM)
    return pl.pallas_call(
        functools.partial(kernel, n_depth, n_tile),
        out_shape=pltpu.VMEM((4, rows, W), f32),
        in_specs=[pl.BlockSpec(memory_space=pl.ANY)] * 4,
        out_specs=vmem,
        scratch_shapes=[
            pltpu.VMEM((chunks + 2, planes, rows, W), f32),
            pltpu.VMEM((chunks + 2, planes, rows, W), f32),
            pltpu.VMEM((chunks, planes, rows + 16, W), f32),
            pltpu.VMEM((chunks, planes + 16, rows + 8, W), f32),
            pltpu.VMEM((chunks + 2, planes + 8, rows + 8, W), f32),
            pltpu.VMEM((chunks, planes + 8, rows, W), f32),
            pltpu.VMEM((chunks, planes, rows + 16, W), f32),
            pltpu.VMEM((chunks, 4, planes, rows, W), f32),
            pltpu.VMEM((chunks, 4, rows, W), f32),
            pltpu.VMEM((chunks, 4, rows, W), f32),
            pltpu.VMEM((4, 2, 8, W), f32),
            pltpu.VMEM((8, W), jnp.int32),
            pltpu.VMEM((2, 6 * W, W), jnp.bfloat16),
            pltpu.VMEM(colour_palette.shape, f32),
            pltpu.VMEM(opacity_palette.shape, f32),
            pltpu.VMEM(tf_index.shape, jnp.int32),
            pltpu.SemaphoreType.DMA((2, chunks)),
            pltpu.SemaphoreType.DMA((3,)),
            pltpu.SemaphoreType.REGULAR((3, 2)),
            pltpu.SemaphoreType.DMA((4, 2, chunks)),
            pltpu.SemaphoreType.DMA((4, 2, chunks)),
            pltpu.SemaphoreType.DMA((chunks,)),
            pltpu.SemaphoreType.DMA((chunks,)),
        ],
        compiler_params=pltpu.CompilerParams(
            collective_id=0,
            has_side_effects=True,
            vmem_limit_bytes=56 * 1024 * 1024,
        ),
    )(fields, colour_palette, opacity_palette, tf_index)


def solution(mesh):
    placed = (P(None, "depth", "tile", None), P(), P(), P())
    return jax.shard_map(
        functools.partial(local, mesh.shape["depth"], mesh.shape["tile"]),
        mesh=mesh,
        in_specs=placed,
        out_specs=P(None, "tile", "depth"),
        check_vma=False,
    )
```
